256 devices in a mesh: tm: 8 (over z_lo, core), sub: 32 (over z_hi, y, x).
Axes of the slice: x: 4, y: 4, z: 8 (z_hi: 2, z_lo: 4; z = z_hi * 4 + z_lo), core: 2. Of those that a mesh axis runs over, the one named last changes fastest.
Arguments:
- field_grads: bfloat16 [8, 3, 1024, 128, 128], P('tm', None, None, 'sub'), may hold values from -6 to 6
- model: float32 [8, 128, 128], P('tm', 'sub'), may hold values from -6 to 6
- observed: float32 [8, 1024, 1024], P('tm', 'sub'), may hold values from -6 to 6
- data_weight: float32 [8, 1024, 1024], P('tm', 'sub'), may hold values from 0.3 to 3
Outputs:
- misfit: float32 [8, 1024, 1024], P('tm', 'sub')
- gradient: float32 [8, 128, 128], P('tm', 'sub')
The draws below stay inside these ranges and needn't reach their ends.
All inputs are finite; a program needn't handle non-finite values.
Results may differ from the reference program's by a relative error of at most 0.0021.
Values may be sent and summed in bfloat16 or wider, within the bound.
A program may use at most 64 MiB of HBM per device.

```python
import math
import jax
import jax.numpy as jnp
from jax import lax

E = 1024
GY = 128
NT = 8
GX = 128
NCELL = 16384


def block_scale(rng, shape, pieces, least, largest):
    factor_of = 1.0
    for position, parts in pieces:
        draws = jax.random.uniform(jax.random.fold_in(jax.random.fold_in(rng, 6), position), (parts,), jnp.float32, least / len(pieces), largest / len(pieces))
        factor_of = factor_of * jnp.repeat(jnp.exp(draws), shape[position] // parts).reshape((-1,) + (1,) * (len(shape) - 1 - position))
    return factor_of


def centred(own_key, dims, scale, reach, split=(), kind=jnp.bfloat16):
    result = scale * jax.random.normal(own_key, dims, jnp.float32)
    if split:
        result = result * block_scale(own_key, dims, split, -0.22, 0.18)
    return jnp.clip(result, -reach, reach).astype(kind)


def setup_inputs(seed: int = 0) -> dict:
    splits = jax.random.split(jax.random.key(seed), 5)
    field_grads = centred(splits[0], (NT, 3, E, GX, GY), 1.0, 6.0, ((0, 8), (3, 32)))
    model = centred(splits[1], (NT, GX, GY), 1.0, 6.0, ((0, 8), (1, 32)), jnp.float32)
    observed = centred(splits[2], (NT, E, E), 1.0, 6.0, ((0, 8), (1, 32)), jnp.float32)
    data_weight = jnp.clip(jnp.exp(math.log(3.0) - 2.3025851 * jax.random.uniform(splits[3], (NT, E, E), jnp.float32) ** block_scale(splits[3], (NT, E, E), ((0, 8), (1, 32)), -0.2, 0.2)), 0.3, 3.0)
    return dict(field_grads=field_grads, model=model, observed=observed, data_weight=data_weight)


def one_time(grads_t, model_t, observed_t, weight_t):
    grads_flat = grads_t.reshape(3, E, NCELL)
    cells = model_t.reshape(NCELL)
    scale = 1.0 / jnp.sqrt(jnp.float32(3 * NCELL))
    predicted = jnp.zeros((E, E), jnp.float32)
    for k in range(3):
        weighted = (grads_flat[k].astype(jnp.float32) * cells).astype(jnp.bfloat16)
        predicted = predicted + lax.dot_general(weighted, grads_flat[k], (((1,), (1,)), ((), ())), preferred_element_type=jnp.float32)
    predicted = predicted * scale
    misfit = weight_t * (predicted - observed_t)
    back = (weight_t * misfit).astype(jnp.bfloat16)
    adjoint = jnp.zeros((NCELL,), jnp.float32)
    for k in range(3):
        product = jnp.dot(back, grads_flat[k], preferred_element_type=jnp.float32)
        adjoint = adjoint + lax.optimization_barrier(jnp.sum(grads_flat[k].astype(jnp.float32) * product, axis=0))
    return (misfit, (adjoint * scale).reshape(GX, GY))

def reference(field_grads, model, observed, data_weight):
    misfits = []
    adjoints = []
    for t in range(NT):
        misfit_t, adjoint_t = one_time(field_grads[t], model[t], observed[t], data_weight[t])
        misfits.append(misfit_t)
        adjoints.append(adjoint_t)
    misfit = jnp.stack(misfits)
    adjoint = jnp.stack(adjoints)
    padded = jnp.pad(model, 1)
    beside = padded[2:, 1:-1, 1:-1] + padded[:-2, 1:-1, 1:-1]
    beside = beside + padded[1:-1, 2:, 1:-1] + padded[1:-1, :-2, 1:-1]
    beside = beside + padded[1:-1, 1:-1, 2:] + padded[1:-1, 1:-1, :-2]
    gradient = adjoint + 6.0 * model - beside
    return (misfit, gradient)
```

```python
import jax
import jax.numpy as jnp
from jax import lax
from jax.experimental import pallas as pl
from jax.experimental.pallas import tpu as pltpu
from jax.sharding import PartitionSpec as P

MESH = pl.DeviceIdType.MESH
F32 = jnp.float32
BF16 = jnp.bfloat16
NX = 4
NY = 4
NZ = 2


def remote(src, dst, send, recv, peer):
    return pltpu.make_async_remote_copy(
        src_ref=src,
        dst_ref=dst,
        send_sem=send,
        recv_sem=recv,
        device_id=peer,
        device_id_type=MESH,
    )


def kernel(
    grads,
    weighted,
    model,
    observed,
    weight,
    misfit_out,
    gradient_out,
    send1,
    recv1,
    acc1,
    recv2,
    acc2,
    recv3,
    gather_a,
    gather_b,
    total,
    faces,
    s1,
    r1,
    s2,
    r2,
    s3,
    r3,
    sf,
    rf,
):
    electrodes, terms = grads.shape
    half = electrodes // 2
    own = misfit_out.shape[1]
    group = NZ * own
    chunk = 4 * group
    cells = terms // 3
    parts = NX * NY * NZ
    tm = lax.axis_index("tm")
    sub = lax.axis_index("sub")
    times = lax.axis_size("tm")
    x = lax.rem(sub, NX)
    y = lax.rem(sub // NX, NY)
    z = sub // (NX * NY)

    def at(zz, yy, xx):
        return {"sub": (zz * NY + yy) * NX + xx}

    def x_peer(d):
        return at(z, y, lax.rem(x + d, NX))

    def y_peer(d):
        return at(z, lax.rem(y + d, NY), x)

    z_peer = at(1 - z, y, x)
    beside = (
        {"tm": lax.rem(tm + 1, times)},
        {"tm": lax.rem(tm + times - 1, times)},
        {"sub": lax.rem(sub + 1, parts)},
        {"sub": lax.rem(sub + parts - 1, parts)},
    )

    barrier = pltpu.get_barrier_semaphore()
    peers = [x_peer(d) for d in (1, 2, 3)] + [y_peer(d) for d in (1, 2, 3)]
    peers += [z_peer] + list(beside)
    for peer in peers:
        pl.semaphore_signal(barrier, inc=1, device_id=peer, device_id_type=MESH)
    pl.semaphore_wait(barrier, len(peers))

    face_copies = [
        remote(model.at[0], faces.at[n], sf.at[n], rf.at[n], peer)
        for n, peer in enumerate(beside)
    ]
    for copy in face_copies:
        copy.start()

    def rows_of(yy, xx, zz):
        return pl.ds(pl.multiple_of(((zz * NY + yy) * NX + xx) * own, own), own)

    def part(pieces, columns):
        rows = jnp.concatenate([weighted[p, :] for p in pieces], axis=0)
        return lax.dot_general(
            rows, grads[columns, :], (((1,), (1,)), ((), ())), preferred_element_type=F32
        )

    def part_a(xx):
        pieces = [rows_of(yy, xx, zz) for yy in range(NY) for zz in range(NZ)]
        return part(pieces, slice(0, half))

    def part_b(yy):
        pieces = [rows_of(yy, xx, zz) for xx in range(NX) for zz in range(NZ)]
        return part(pieces, slice(half, electrodes))

    first = {}
    for d in (2, 1, 3):
        send1[0, d - 1] = part_a(lax.rem(x + d, NX)).astype(BF16)
        first[0, d] = remote(send1.at[0, d - 1], recv1.at[0, d - 1], s1.at[0, d - 1], r1.at[0, d - 1], x_peer(d))
        first[0, d].start()
        send1[1, d - 1] = part_b(lax.rem(y + d, NY)).astype(BF16)
        first[1, d] = remote(send1.at[1, d - 1], recv1.at[1, d - 1], s1.at[1, d - 1], r1.at[1, d - 1], y_peer(d))
        first[1, d].start()
    acc1[0] = part_a(x)
    acc1[1] = part_b(y)

    second = {}
    for h, mine, peer_of in ((0, y, y_peer), (1, x, x_peer)):
        for d in (1, 3, 2):
            first[h, d].wait_recv()
        acc1[h] += recv1[h, 0].astype(F32) + recv1[h, 1].astype(F32) + recv1[h, 2].astype(F32)
        for d in (2, 1, 3):
            other = lax.rem(mine + d, 4)
            src = acc1.at[h, pl.ds(pl.multiple_of(other * group, group), group), :]
            second[h, d] = remote(src, recv2.at[h, d - 1], s2.at[h, d - 1], r2.at[h, d - 1], peer_of(d))
            second[h, d].start()
    third = {}
    for h, mine in ((0, y), (1, x)):
        for d in (1, 3, 2):
            second[h, d].wait_recv()
        kept = acc1[h, pl.ds(pl.multiple_of(mine * group, group), group), :]
        acc2[h] = kept + recv2[h, 0] + recv2[h, 1] + recv2[h, 2]
        src = acc2.at[h, pl.ds(pl.multiple_of((1 - z) * own, own), own), :]
        third[h] = remote(src, recv3.at[h], s3.at[h], r3.at[h], z_peer)
        third[h].start()

    scale = 1.0 / jnp.sqrt(F32(cells * 3 * parts))
    gather = (gather_a, gather_b)
    slots = ((y, x), (x, y))
    copies = []
    level0 = {}
    for h in range(2):
        third[h].wait_recv()
        columns = slice(h * half, (h + 1) * half)
        summed = acc2[h, pl.ds(pl.multiple_of(z * own, own), own), :] + recv3[h]
        w = weight[0, :, columns]
        misfit = w * (summed * scale - observed[0, :, columns])
        misfit_out[0, :, columns] = misfit
        block = gather[h].at[slots[h][0], slots[h][1], z]
        block[...] = (w * misfit).astype(BF16)
        level0[h] = remote(block, block, s3.at[2 + h], r3.at[2 + h], z_peer)
        level0[h].start()

    level1 = {}
    for h, peer_of in ((0, x_peer), (1, y_peer)):
        level0[h].wait_recv()
        for d in (2, 1, 3):
            block = gather[h].at[slots[h][0], slots[h][1]]
            level1[h, d] = remote(block, block, s2.at[2 + h, d - 1], r2.at[2 + h, d - 1], peer_of(d))
            level1[h, d].start()
    level2 = {}
    for h, peer_of in ((0, y_peer), (1, x_peer)):
        for d in (1, 3, 2):
            level1[h, d].wait_recv()
        for d in (2, 1, 3):
            block = gather[h].at[slots[h][0]]
            level2[h, d] = remote(block, block, s1.at[2 + h, d - 1], r1.at[2 + h, d - 1], peer_of(d))
            level2[h, d].start()

    total[...] = jnp.zeros_like(total)

    def add(h, slot):
        back = gather[h][slot].reshape(chunk, half)
        product = jnp.dot(back, grads[h * half : (h + 1) * half, :], preferred_element_type=F32)
        outer = range(4)
        if h == 0:
            pieces = [rows_of(slot, xx, zz) for xx in outer for zz in range(NZ)]
        else:
            pieces = [rows_of(yy, slot, zz) for yy in outer for zz in range(NZ)]
        rows = jnp.concatenate([grads[p, :] for p in pieces], axis=0)
        terms_of = product * rows.astype(F32)
        total[...] += jnp.sum(terms_of.reshape(chunk // 8, 8, terms), axis=0)

    add(0, y)
    add(1, x)
    for d in (1, 3, 2):
        for h, mine in ((0, y), (1, x)):
            level2[h, d].wait_recv()
            add(h, lax.rem(mine + 4 - d, 4))

    for copy in face_copies:
        copy.wait_recv()
    centre = model[0]
    lane = lax.broadcasted_iota(jnp.int32, centre.shape, 1)
    width = centre.shape[1]
    row = lax.broadcasted_iota(jnp.int32, centre.shape, 0)
    height = centre.shape[0]
    nil = jnp.zeros_like(centre)
    before_t = jnp.where(tm > 0, faces[0], nil)
    after_t = jnp.where(tm < times - 1, faces[1], nil)
    before_s = jnp.where(sub > 0, faces[2], nil)
    after_s = jnp.where(sub < parts - 1, faces[3], nil)
    near = after_t + before_t
    near = near + jnp.concatenate([centre[1:], after_s[:1]], axis=0)
    near = near + jnp.concatenate([before_s[height - 1 :], centre[: height - 1]], axis=0)
    near = near + jnp.where(lane == width - 1, 0.0, pltpu.roll(centre, width - 1, 1))
    near = near + jnp.where(lane == 0, 0.0, pltpu.roll(centre, 1, 1))
    smooth = 6.0 * centre - near
    flat = jnp.sum(total[...], axis=0, keepdims=True)
    flat = (flat[:, :cells] + flat[:, cells : 2 * cells] + flat[:, 2 * cells :]) * scale
    for j in range(height):
        gradient_out[0, j : j + 1, :] = flat[:, j * width : (j + 1) * width] + smooth[j : j + 1]

    for copy in face_copies:
        copy.wait_send()
    for sent in (first, second, third, level0, level1, level2):
        for copy in sent.values():
            copy.wait_send()


def body(field_grads, model, observed, data_weight):
    electrodes = field_grads.shape[2]
    columns = field_grads.shape[3]
    width = field_grads.shape[4]
    cells = columns * width
    own = observed.shape[1]
    half = electrodes // 2
    group = NZ * own
    chunk = 4 * group
    grads = jnp.transpose(field_grads[0], (1, 0, 2, 3)).reshape(electrodes, 3 * cells)
    m = jnp.tile(model.reshape(1, cells), (1, 3))
    weighted = (grads.astype(F32) * m).astype(BF16)
    dma = pltpu.SemaphoreType.DMA
    vmem = pl.BlockSpec(memory_space=pltpu.VMEM)
    return pl.pallas_call(
        kernel,
        out_shape=(
            jax.ShapeDtypeStruct(observed.shape, F32),
            jax.ShapeDtypeStruct(model.shape, F32),
        ),
        in_specs=[vmem] * 5,
        out_specs=(vmem, vmem),
        scratch_shapes=[
            pltpu.VMEM((2, 3, chunk, half), BF16),
            pltpu.VMEM((2, 3, chunk, half), BF16),
            pltpu.VMEM((2, chunk, half), F32),
            pltpu.VMEM((2, 3, group, half), F32),
            pltpu.VMEM((2, group, half), F32),
            pltpu.VMEM((2, own, half), F32),
            pltpu.VMEM((4, 4, NZ, own, half), BF16),
            pltpu.VMEM((4, 4, NZ, own, half), BF16),
            pltpu.VMEM((8, 3 * cells), F32),
            pltpu.VMEM((4, columns, width), F32),
            dma((4, 3)),
            dma((4, 3)),
            dma((4, 3)),
            dma((4, 3)),
            dma((4,)),
            dma((4,)),
            dma((4,)),
            dma((4,)),
        ],
        compiler_params=pltpu.CompilerParams(
            collective_id=0, has_side_effects=True, vmem_limit_bytes=48 * 1024 * 1024
        ),
    )(grads, weighted, model, observed, data_weight)


def solution(mesh):
    return jax.shard_map(
        body,
        mesh=mesh,
        in_specs=(
            P("tm", None, None, "sub", None),
            P("tm", "sub", None),
            P("tm", "sub", None),
            P("tm", "sub", None),
        ),
        out_specs=(P("tm", "sub", None), P("tm", "sub", None)),
        check_vma=False,
    )
```

```python
import jax
import jax.numpy as jnp
from jax import lax
from jax.experimental import pallas as pl
from jax.experimental.pallas import tpu as pltpu
from jax.sharding import PartitionSpec as P

MESH = pl.DeviceIdType.MESH
F32 = jnp.float32
BF16 = jnp.bfloat16
N = 4
NZ = 2
LANES = 128
FAR_FIRST = (2, 1, 3)
NEAR_FIRST = (1, 3, 2)


def kernel(
    fields,
    model,
    observed,
    weight,
    misfit_out,
    gradient_out,
    raw,
    grads,
    weighted,
    pairs_a,
    pairs_b,
    send_a,
    send_b,
    recv_a,
    recv_b,
    acc_a,
    acc_b,
    recv_a2,
    recv_b2,
    z_send,
    z_recv,
    gather_a,
    gather_b,
    data,
    data_y,
    data_t,
    data_x,
    data_u,
    data_z,
    post,
    post_y,
    post_t,
    post_x,
    potential,
    total,
    faces,
    load_sem,
    send_sem,
    recv_sem,
):
    electrodes, terms = grads.shape
    half = electrodes // 2
    own = misfit_out.shape[1]
    tile = N * own
    cells = terms // 3
    parts = N * N * NZ
    tm = lax.axis_index("tm")
    sub = lax.axis_index("sub")
    times = lax.axis_size("tm")
    x = lax.rem(sub, N)
    y = lax.rem(sub // N, N)
    z = sub // (N * N)

    def at(zz, yy, xx):
        return {"sub": (zz * N + yy) * N + xx}

    def x_peer(d):
        return at(z, y, lax.rem(x + d, N))

    def y_peer(d):
        return at(z, lax.rem(y + d, N), x)

    z_peer = at(1 - z, y, x)
    beside = (
        {"tm": lax.rem(tm + 1, times)},
        {"tm": lax.rem(tm + times - 1, times)},
        {"sub": lax.rem(sub + 1, parts)},
        {"sub": lax.rem(sub + parts - 1, parts)},
    )
    sent = []

    def start(src, dst, peer):
        n = len(sent)
        copy = pltpu.make_async_remote_copy(
            src_ref=src,
            dst_ref=dst,
            send_sem=send_sem.at[n],
            recv_sem=recv_sem.at[n],
            device_id=peer,
            device_id_type=MESH,
        )
        sent.append(copy)
        copy.start()
        return copy

    loads = [pltpu.make_async_copy(fields.at[0, k], raw.at[k], load_sem.at[k]) for k in range(3)]
    for load in loads:
        load.start()

    barrier = pltpu.get_barrier_semaphore()
    peers = [x_peer(d) for d in FAR_FIRST] + [y_peer(d) for d in FAR_FIRST]
    peers += [z_peer] + list(beside)
    for peer in peers:
        pl.semaphore_signal(barrier, inc=1, device_id=peer, device_id_type=MESH)

    for n in range(2 * N):
        columns = slice(n * LANES, (n + 1) * LANES)
        e = weight[0, :, columns] * weight[0, :, columns]
        other = z if n < N else 1 - z
        data[n % N, other] = e
        data[n % N, 2 + other] = e * observed[0, :, columns]
    pl.semaphore_wait(barrier, len(peers))

    def begin_y(box, box_y):
        copies = [
            start(box.at[lax.rem(y + d, N)], box_y.at[y], y_peer(d)) for d in FAR_FIRST
        ]
        box_y[y] = box[y]
        return copies

    def begin_x(copies, box_y, box_t, box_x):
        for copy in copies:
            copy.wait_recv()
        for q in range(box_y.shape[1]):
            square = jnp.concatenate([box_y[n, q] for n in range(N)], axis=0)
            turned = square.T
            for n in range(N):
                box_t[n, q] = turned[n * own : (n + 1) * own]
        copies = [
            start(box_t.at[lax.rem(x + d, N)], box_x.at[x], x_peer(d)) for d in FAR_FIRST
        ]
        box_x[x] = box_t[x]
        return copies

    lane_block = lax.broadcasted_iota(jnp.int32, (own, LANES), 1) // own

    def mirrored(box_x, q, t):
        result = None
        for n in range(N):
            moved = box_x[n, q]
            if n != t:
                moved = pltpu.roll(moved, ((n - t) % N) * own, 1)
            result = moved if result is None else jnp.where(lane_block == n, moved, result)
        return result

    data_copies = begin_y(data, data_y)
    face_copies = [start(model.at[0], faces.at[n], peer) for n, peer in enumerate(beside)]

    cell_row = jnp.concatenate([model[0, j : j + 1, :] for j in range(model.shape[1])], axis=1)

    def lay_out(k):
        loads[k].wait()
        columns = slice(k * cells, (k + 1) * cells)
        for n in range(4):
            rows = slice(n * 256, (n + 1) * 256)
            flat = raw[k, rows].reshape(256, cells)
            grads[rows, columns] = flat
            weighted[rows, columns] = (flat.astype(F32) * cell_row).astype(BF16)

    def product(rows, columns):
        return lax.dot_general(
            weighted[rows, :], grads[columns, :], (((1,), (1,)), ((), ())), preferred_element_type=F32
        )

    lay_out(0)
    data_copies = begin_x(data_copies, data_y, data_t, data_x)
    lay_out(1)
    lay_out(2)

    for b in range(2):
        block = product(slice(b * 256, (b + 1) * 256), slice(half, electrodes))
        for n in range(2):
            for xx in range(N):
                piece = block[n * tile + xx * own : n * tile + (xx + 1) * own]
                pairs_a[xx, 2 * b + n] = piece
                send_a[xx, 2 * b + n] = piece.astype(BF16)
    first_a = [start(send_a.at[lax.rem(x + d, N)], recv_a.at[d - 1], x_peer(d)) for d in FAR_FIRST]

    def keep(block, block_row, block_column, row, column, place):
        r = (row - block_row) * LANES
        c = (column - block_column) * LANES
        piece = block[r : r + LANES, c : c + LANES]
        columns = slice(place * LANES, (place + 1) * LANES)
        pairs_b[row, :, columns] = piece
        send_b[row, :, columns] = piece.astype(BF16)

    for b in range(2):
        upper = product(slice(b * 256, (b + 1) * 256), slice(b * 256, half))
        lower = product(
            slice(half + b * 256, half + (b + 1) * 256), slice(half, half + (b + 1) * 256)
        )
        for row in (2 * b, 2 * b + 1):
            for column in range(N):
                if column >= row:
                    keep(upper, 2 * b, 2 * b, row, column, column)
                else:
                    keep(lower, 2 * b, 0, row, column, column)
            keep(lower, 2 * b, 0, row, row, N)
    first_b = [start(send_b.at[lax.rem(y + d, N)], recv_b.at[d - 1], y_peer(d)) for d in FAR_FIRST]

    for copy in data_copies:
        copy.wait_recv()
    low = z == 0
    nil = jnp.zeros((own, LANES), F32)
    for v in range(2):
        for t in range(N):
            data_u[v, t] = jnp.where(low, data[t, 2 * v + 1], mirrored(data_x, 2 * v + 1, t))
            direct = data[t, 2 * v]
            both = direct + mirrored(data_x, 2 * v, t)
            inside = jnp.where(low, t > y, t < y)
            corner = jnp.logical_and(low, y == t)
            data_u[v, N + t] = jnp.where(inside, both, jnp.where(corner, direct, nil))
        data_u[v, 2 * N] = jnp.where(low, nil, data[y, 2 * v])
    data_copy = start(data_u, data_z, z_peer)

    def arrived(copies, box):
        for copy in copies:
            copy.wait_recv()
        return box[0].astype(F32) + box[1].astype(F32) + box[2].astype(F32)

    acc_a[...] = pairs_a[x] + arrived(first_a, recv_a)
    second_a = [start(acc_a.at[lax.rem(y + d, N)], recv_a2.at[d - 1], y_peer(d)) for d in FAR_FIRST]
    acc_b[...] = (pairs_b[y] + arrived(first_b, recv_b)).reshape(acc_b.shape)
    second_b = [start(acc_b.at[lax.rem(x + d, N)], recv_b2.at[d - 1], x_peer(d)) for d in FAR_FIRST]

    sums = []
    third = []
    for v, (acc, mine, copies, box) in enumerate(
        ((acc_a, y, second_a, recv_a2), (acc_b, x, second_b, recv_b2))
    ):
        summed = acc[mine] + arrived(copies, box)
        potential[:, v * half : v * half + summed.shape[1]] = summed
        z_send[v, :, : summed.shape[1]] = summed.astype(BF16)
        third.append(start(z_send.at[v], z_recv.at[v], z_peer))

    scale = 1.0 / jnp.sqrt(F32(cells * 3 * parts))
    data_copy.wait_recv()

    def finish(v, tiles):
        third[v].wait_recv()
        for t in tiles:
            columns = slice(t * LANES, (t + 1) * LANES)
            inner = slice((t - v * N) * LANES, (t - v * N + 1) * LANES)
            value = (potential[:, columns] + z_recv[v, :, inner].astype(F32)) * scale
            potential[:, columns] = value
            residual = (data_u[0, t] + data_z[0, t]) * value - (data_u[1, t] + data_z[1, t])
            if v == 0:
                gather_a[x, y, :, inner] = residual.astype(BF16)
                post[t, 1] = value
            else:
                gather_b[y, x, :, inner] = residual.astype(BF16)
                if t < 2 * N:
                    post[t - N, 0] = value

    finish(0, range(N))
    level_a = [start(gather_a.at[x, y], gather_a.at[x, y], y_peer(d)) for d in FAR_FIRST]
    finish(1, range(N, 2 * N + 1))
    level_b = [start(gather_b.at[y, x], gather_b.at[y, x], x_peer(d)) for d in FAR_FIRST]
    post_copies = begin_y(post, post_y)
    for copy in level_a:
        copy.wait_recv()
    last_a = {d: start(gather_a.at[x], gather_a.at[x], x_peer(d)) for d in FAR_FIRST}
    for copy in level_b:
        copy.wait_recv()
    last_b = {d: start(gather_b.at[y], gather_b.at[y], y_peer(d)) for d in FAR_FIRST}
    post_copies = begin_x(post_copies, post_y, post_t, post_x)

    total[...] = jnp.zeros_like(total)

    def collect(matrix, columns, rows):
        made = jnp.dot(matrix, grads[columns, :], preferred_element_type=F32)
        made = made * rows.astype(F32)
        total[...] += jnp.sum(made.reshape(tile // 8, 8, terms), axis=0)

    def at_rows(first, count):
        return pl.ds(pl.multiple_of(first, count), count)

    def add_a(xx):
        rows = jnp.concatenate([grads[at_rows(yy * tile + xx * own, own), :] for yy in range(N)], axis=0)
        collect(gather_a[xx].reshape(tile, half), slice(half, electrodes), rows)

    def add_b(yy):
        matrix = gather_b[yy].reshape(tile, half + LANES)
        tiles = [matrix[:, t * LANES : (t + 1) * LANES] for t in range(N + 1)]
        none = jnp.zeros_like(tiles[0])
        upper = [jnp.where(yy <= t, tiles[t], none) for t in range(N)]
        lower = [
            jnp.where(yy > t, tiles[t], jnp.where(yy == t, tiles[N], none)) for t in range(N)
        ]
        collect(jnp.concatenate(upper, axis=1), slice(0, half), grads[at_rows(yy * tile, tile), :])
        collect(
            jnp.concatenate(lower, axis=1),
            slice(half, electrodes),
            grads[at_rows(half + yy * tile, tile), :],
        )

    add_a(x)
    add_b(y)

    for copy in post_copies:
        copy.wait_recv()
    for n in range(2 * N):
        columns = slice(n * LANES, (n + 1) * LANES)
        t = n % N
        between = potential[:, t * LANES : (t + 1) * LANES]
        within = potential[:, half + t * LANES : half + (t + 1) * LANES]
        corner = potential[:, 2 * half : 2 * half + LANES]
        turned = mirrored(post_x, 0, t)
        upper = jnp.where(y <= t, within, turned)
        lower = jnp.where(y > t, within, jnp.where(y == t, corner, turned))
        mine = jnp.where(low, upper, lower)
        others = jnp.where(low, between, mirrored(post_x, 1, t))
        here = low if n < N else z == 1
        value = jnp.where(here, mine, others)
        misfit_out[0, :, columns] = weight[0, :, columns] * (value - observed[0, :, columns])

    for d in NEAR_FIRST:
        last_a[d].wait_recv()
        add_a(lax.rem(x + N - d, N))
        last_b[d].wait_recv()
        add_b(lax.rem(y + N - d, N))

    for copy in face_copies:
        copy.wait_recv()
    centre = model[0]
    height, width = centre.shape
    lane = lax.broadcasted_iota(jnp.int32, centre.shape, 1)
    zero = jnp.zeros_like(centre)
    before_t = jnp.where(tm > 0, faces[0], zero)
    after_t = jnp.where(tm < times - 1, faces[1], zero)
    before_s = jnp.where(sub > 0, faces[2], zero)
    after_s = jnp.where(sub < parts - 1, faces[3], zero)
    near = after_t + before_t
    near = near + jnp.concatenate([centre[1:], after_s[:1]], axis=0)
    near = near + jnp.concatenate([before_s[height - 1 :], centre[: height - 1]], axis=0)
    near = near + jnp.where(lane == width - 1, 0.0, pltpu.roll(centre, width - 1, 1))
    near = near + jnp.where(lane == 0, 0.0, pltpu.roll(centre, 1, 1))
    smooth = 6.0 * centre - near
    flat = jnp.sum(total[...], axis=0, keepdims=True)
    flat = (flat[:, :cells] + flat[:, cells : 2 * cells] + flat[:, 2 * cells :]) * scale
    for j in range(height):
        gradient_out[0, j : j + 1, :] = flat[:, j * width : (j + 1) * width] + smooth[j : j + 1]

    for copy in sent:
        copy.wait_send()


def body(field_grads, model, observed, data_weight):
    electrodes = field_grads.shape[2]
    columns = field_grads.shape[3]
    width = field_grads.shape[4]
    terms = 3 * columns * width
    own = observed.shape[1]
    half = electrodes // 2
    tile = N * own
    wide = half + LANES
    dma = pltpu.SemaphoreType.DMA
    vmem = pl.BlockSpec(memory_space=pltpu.VMEM)
    return pl.pallas_call(
        kernel,
        out_shape=(
            jax.ShapeDtypeStruct(observed.shape, F32),
            jax.ShapeDtypeStruct(model.shape, F32),
        ),
        in_specs=[pl.BlockSpec(memory_space=pl.ANY)] + [vmem] * 3,
        out_specs=(vmem, vmem),
        scratch_shapes=[
            pltpu.VMEM((3, electrodes, columns, width), BF16),
            pltpu.VMEM((electrodes, terms), BF16),
            pltpu.VMEM((electrodes, terms), BF16),
            pltpu.VMEM((N, N, own, half), F32),
            pltpu.VMEM((N, tile, wide), F32),
            pltpu.VMEM((N, N, own, half), BF16),
            pltpu.VMEM((N, tile, wide), BF16),
            pltpu.VMEM((3, N, own, half), BF16),
            pltpu.VMEM((3, tile, wide), BF16),
            pltpu.VMEM((N, own, half), F32),
            pltpu.VMEM((N, own, wide), F32),
            pltpu.VMEM((3, own, half), F32),
            pltpu.VMEM((3, own, wide), F32),
            pltpu.VMEM((2, own, wide), BF16),
            pltpu.VMEM((2, own, wide), BF16),
            pltpu.VMEM((N, N, own, half), BF16),
            pltpu.VMEM((N, N, own, wide), BF16),
            pltpu.VMEM((N, 4, own, LANES), F32),
            pltpu.VMEM((N, 4, own, LANES), F32),
            pltpu.VMEM((N, 4, own, LANES), F32),
            pltpu.VMEM((N, 4, own, LANES), F32),
            pltpu.VMEM((2, 2 * N + 1, own, LANES), F32),
            pltpu.VMEM((2, 2 * N + 1, own, LANES), F32),
            pltpu.VMEM((N, 2, own, LANES), F32),
            pltpu.VMEM((N, 2, own, LANES), F32),
            pltpu.VMEM((N, 2, own, LANES), F32),
            pltpu.VMEM((N, 2, own, LANES), F32),
            pltpu.VMEM((own, 2 * half + LANES), F32),
            pltpu.VMEM((8, terms), F32),
            pltpu.VMEM((4, columns, width), F32),
            dma((3,)),
            dma((48,)),
            dma((48,)),
        ],
        compiler_params=pltpu.CompilerParams(
            collective_id=0, has_side_effects=True, vmem_limit_bytes=48 * 1024 * 1024
        ),
    )(field_grads, model, observed, data_weight)


def solution(mesh):
    return jax.shard_map(
        body,
        mesh=mesh,
        in_specs=(
            P("tm", None, None, "sub", None),
            P("tm", "sub", None),
            P("tm", "sub", None),
            P("tm", "sub", None),
        ),
        out_specs=(P("tm", "sub", None), P("tm", "sub", None)),
        check_vma=False,
    )
```

```python
import jax
import jax.numpy as jnp
from jax import lax
from jax.experimental import pallas as pl
from jax.experimental.pallas import tpu as pltpu
from jax.sharding import PartitionSpec as P

MESH = pl.DeviceIdType.MESH
F32 = jnp.float32
BF16 = jnp.bfloat16
N = 4
NZ = 2
LANES = 128
FAR_FIRST = (2, 1, 3)
NEAR_FIRST = (1, 3, 2)


def kernel(
    fields,
    model_in,
    observed_in,
    weight_in,
    misfit_out,
    gradient_out,
    model,
    observed,
    weight,
    raw,
    grads,
    weighted,
    pairs_a,
    pairs_b,
    send_a,
    send_b,
    recv_a,
    recv_b,
    acc_a,
    acc_b,
    recv_a2,
    recv_b2,
    z_send,
    z_recv,
    gather_a,
    gather_b,
    data,
    data_y,
    data_t,
    data_x,
    data_u,
    data_b,
    data_z,
    post,
    post_y,
    post_t,
    post_x,
    potential,
    total,
    faces,
    load_sem,
    send_sem,
    recv_sem,
):
    electrodes, terms = grads.shape
    half = electrodes // 2
    own = misfit_out.shape[1]
    tile = N * own
    cells = terms // 3
    parts = N * N * NZ
    tm = lax.axis_index("tm")
    sub = lax.axis_index("sub")
    times = lax.axis_size("tm")
    x = lax.rem(sub, N)
    y = lax.rem(sub // N, N)
    z = sub // (N * N)

    def at(zz, yy, xx):
        return {"sub": (zz * N + yy) * N + xx}

    def x_peer(d):
        return at(z, y, lax.rem(x + d, N))

    def y_peer(d):
        return at(z, lax.rem(y + d, N), x)

    z_peer = at(1 - z, y, x)
    beside = (
        {"tm": lax.rem(tm + 1, times)},
        {"tm": lax.rem(tm + times - 1, times)},
        {"sub": lax.rem(sub + 1, parts)},
        {"sub": lax.rem(sub + parts - 1, parts)},
    )
    sent = []

    def start(src, dst, peer):
        n = len(sent)
        copy = pltpu.make_async_remote_copy(
            src_ref=src,
            dst_ref=dst,
            send_sem=send_sem.at[n],
            recv_sem=recv_sem.at[n],
            device_id=peer,
            device_id_type=MESH,
        )
        sent.append(copy)
        copy.start()
        return copy

    loads = [pltpu.make_async_copy(fields.at[0, k], raw.at[k], load_sem.at[k]) for k in range(3)]
    inputs = [
        pltpu.make_async_copy(src, dst, load_sem.at[3 + n])
        for n, (src, dst) in enumerate(
            ((weight_in, weight), (observed_in, observed), (model_in, model))
        )
    ]
    for load in inputs + loads:
        load.start()

    barrier = pltpu.get_barrier_semaphore()
    peers = [x_peer(d) for d in FAR_FIRST] + [y_peer(d) for d in FAR_FIRST]
    peers += [z_peer] + list(beside)
    for peer in peers:
        pl.semaphore_signal(barrier, inc=1, device_id=peer, device_id_type=MESH)

    for load in inputs:
        load.wait()

    for n in range(2 * N):
        columns = slice(n * LANES, (n + 1) * LANES)
        e = weight[0, :, columns] * weight[0, :, columns]
        other = z if n < N else 1 - z
        data[n % N, other] = e
        data[n % N, 2 + other] = e * observed[0, :, columns]

    def begin_y(box, box_y):
        copies = [
            start(box.at[lax.rem(y + d, N)], box_y.at[y], y_peer(d)) for d in FAR_FIRST
        ]
        box_y[y] = box[y]
        return copies

    def begin_x(copies, box_y, box_t, box_x):
        for copy in copies:
            copy.wait_recv()
        for q in range(box_y.shape[1]):
            square = jnp.concatenate([box_y[n, q] for n in range(N)], axis=0)
            turned = square.T
            for n in range(N):
                box_t[n, q] = turned[n * own : (n + 1) * own]
        copies = [
            start(box_t.at[lax.rem(x + d, N)], box_x.at[x], x_peer(d)) for d in FAR_FIRST
        ]
        box_x[x] = box_t[x]
        return copies

    lane_block = lax.broadcasted_iota(jnp.int32, (own, LANES), 1) // own

    def mirrored(box_x, q, t):
        result = None
        for n in range(N):
            moved = box_x[n, q]
            if n != t:
                moved = pltpu.roll(moved, ((n - t) % N) * own, 1)
            result = moved if result is None else jnp.where(lane_block == n, moved, result)
        return result

    cell_row = jnp.concatenate([model[0, j : j + 1, :] for j in range(model.shape[1])], axis=1)

    def lay_out(k):
        loads[k].wait()
        columns = slice(k * cells, (k + 1) * cells)
        for n in range(4):
            rows = slice(n * 256, (n + 1) * 256)
            flat = raw[k, rows].reshape(256, cells)
            grads[rows, columns] = flat
            weighted[rows, columns] = (flat.astype(F32) * cell_row).astype(BF16)

    def product(rows, columns):
        return lax.dot_general(
            weighted[rows, :], grads[columns, :], (((1,), (1,)), ((), ())), preferred_element_type=F32
        )

    lay_out(0)
    pl.semaphore_wait(barrier, len(peers))
    data_copies = begin_y(data, data_y)
    face_copies = [start(model.at[0], faces.at[n], peer) for n, peer in enumerate(beside)]
    lay_out(1)
    lay_out(2)

    def keep(block, block_row, block_column, row, column, place):
        r = (row - block_row) * LANES
        c = (column - block_column) * LANES
        piece = block[r : r + LANES, c : c + LANES]
        columns = slice(place * LANES, (place + 1) * LANES)
        pairs_b[row, :, columns] = piece
        send_b[row, :, columns] = piece.astype(BF16)

    for b in range(2):
        upper = product(slice(b * 256, (b + 1) * 256), slice(b * 256, half))
        lower = product(
            slice(half + b * 256, half + (b + 1) * 256), slice(half, half + (b + 1) * 256)
        )
        for row in (2 * b, 2 * b + 1):
            for column in range(N):
                if column >= row:
                    keep(upper, 2 * b, 2 * b, row, column, column)
                else:
                    keep(lower, 2 * b, 0, row, column, column)
            keep(lower, 2 * b, 0, row, row, N)
    first_b = [start(send_b.at[lax.rem(y + d, N)], recv_b.at[d - 1], y_peer(d)) for d in FAR_FIRST]

    for b in range(2):
        block = product(slice(b * 256, (b + 1) * 256), slice(half, electrodes))
        for n in range(2):
            for xx in range(N):
                piece = block[n * tile + xx * own : n * tile + (xx + 1) * own]
                pairs_a[xx, 2 * b + n] = piece
                send_a[xx, 2 * b + n] = piece.astype(BF16)
    first_a = [start(send_a.at[lax.rem(x + d, N)], recv_a.at[d - 1], x_peer(d)) for d in FAR_FIRST]
    data_copies = begin_x(data_copies, data_y, data_t, data_x)

    for copy in data_copies:
        copy.wait_recv()
    low = z == 0
    nil = jnp.zeros((own, LANES), F32)
    for v in range(2):
        for t in range(N):
            data_u[v, t] = jnp.where(low, data[t, 2 * v + 1], mirrored(data_x, 2 * v + 1, t))
            direct = data[t, 2 * v]
            both = direct + mirrored(data_x, 2 * v, t)
            inside = jnp.where(low, t > y, t < y)
            corner = jnp.logical_and(low, y == t)
            data_u[v, N + t] = jnp.where(inside, both, jnp.where(corner, direct, nil))
        data_u[v, 2 * N] = jnp.where(low, nil, data[y, 2 * v])
    data_b[...] = data_u[...].astype(BF16)
    data_copy = start(data_b, data_z, z_peer)

    def arrived(copies, box):
        for copy in copies:
            copy.wait_recv()
        return box[0].astype(F32) + box[1].astype(F32) + box[2].astype(F32)

    acc_b[...] = (pairs_b[y] + arrived(first_b, recv_b)).reshape(acc_b.shape)
    second_b = [start(acc_b.at[lax.rem(x + d, N)], recv_b2.at[d - 1], x_peer(d)) for d in FAR_FIRST]
    acc_a[...] = pairs_a[x] + arrived(first_a, recv_a)
    second_a = [start(acc_a.at[lax.rem(y + d, N)], recv_a2.at[d - 1], y_peer(d)) for d in FAR_FIRST]

    sums = []
    third = []
    for v, (acc, mine, copies, box) in enumerate(
        ((acc_a, y, second_a, recv_a2), (acc_b, x, second_b, recv_b2))
    ):
        summed = acc[mine] + arrived(copies, box)
        potential[:, v * half : v * half + summed.shape[1]] = summed
        z_send[v, :, : summed.shape[1]] = summed.astype(BF16)
        third.append(start(z_send.at[v], z_recv.at[v], z_peer))

    scale = 1.0 / jnp.sqrt(F32(cells * 3 * parts))
    data_copy.wait_recv()

    def finish(v, tiles):
        third[v].wait_recv()
        for t in tiles:
            columns = slice(t * LANES, (t + 1) * LANES)
            inner = slice((t - v * N) * LANES, (t - v * N + 1) * LANES)
            value = (potential[:, columns] + z_recv[v, :, inner].astype(F32)) * scale
            potential[:, columns] = value
            factor = data_u[0, t] + data_z[0, t].astype(F32)
            residual = factor * value - (data_u[1, t] + data_z[1, t].astype(F32))
            if v == 0:
                gather_a[x, y, :, inner] = residual.astype(BF16)
                post[t, 1] = value
            else:
                gather_b[y, x, :, inner] = residual.astype(BF16)
                if t < 2 * N:
                    post[t - N, 0] = value

    finish(0, range(N))
    level_a = [start(gather_a.at[x, y], gather_a.at[x, y], y_peer(d)) for d in FAR_FIRST]
    finish(1, range(N, 2 * N + 1))
    level_b = [start(gather_b.at[y, x], gather_b.at[y, x], x_peer(d)) for d in FAR_FIRST]
    post_copies = begin_y(post, post_y)
    for copy in level_a:
        copy.wait_recv()
    last_a = {d: start(gather_a.at[x], gather_a.at[x], x_peer(d)) for d in FAR_FIRST}
    for copy in level_b:
        copy.wait_recv()
    last_b = {d: start(gather_b.at[y], gather_b.at[y], y_peer(d)) for d in FAR_FIRST}
    post_copies = begin_x(post_copies, post_y, post_t, post_x)

    total[...] = jnp.zeros_like(total)

    def collect(matrix, columns, rows):
        made = jnp.dot(matrix, grads[columns, :], preferred_element_type=F32)
        made = made * rows.astype(F32)
        total[...] += jnp.sum(made.reshape(tile // 8, 8, terms), axis=0)

    def at_rows(first, count):
        return pl.ds(pl.multiple_of(first, count), count)

    def add_a(xx):
        rows = jnp.concatenate([grads[at_rows(yy * tile + xx * own, own), :] for yy in range(N)], axis=0)
        collect(gather_a[xx].reshape(tile, half), slice(half, electrodes), rows)

    def add_b(yy):
        matrix = gather_b[yy].reshape(tile, half + LANES)
        tiles = [matrix[:, t * LANES : (t + 1) * LANES] for t in range(N + 1)]
        none = jnp.zeros_like(tiles[0])
        upper = [jnp.where(yy <= t, tiles[t], none) for t in range(N)]
        lower = [
            jnp.where(yy > t, tiles[t], jnp.where(yy == t, tiles[N], none)) for t in range(N)
        ]
        collect(jnp.concatenate(upper, axis=1), slice(0, half), grads[at_rows(yy * tile, tile), :])
        collect(
            jnp.concatenate(lower, axis=1),
            slice(half, electrodes),
            grads[at_rows(half + yy * tile, tile), :],
        )

    add_a(x)
    add_b(y)

    for copy in post_copies:
        copy.wait_recv()
    for n in range(2 * N):
        columns = slice(n * LANES, (n + 1) * LANES)
        t = n % N
        between = potential[:, t * LANES : (t + 1) * LANES]
        within = potential[:, half + t * LANES : half + (t + 1) * LANES]
        corner = potential[:, 2 * half : 2 * half + LANES]
        turned = mirrored(post_x, 0, t)
        upper = jnp.where(y <= t, within, turned)
        lower = jnp.where(y > t, within, jnp.where(y == t, corner, turned))
        mine = jnp.where(low, upper, lower)
        others = jnp.where(low, between, mirrored(post_x, 1, t))
        here = low if n < N else z == 1
        value = jnp.where(here, mine, others)
        misfit_out[0, :, columns] = weight[0, :, columns] * (value - observed[0, :, columns])

    for d in NEAR_FIRST:
        last_a[d].wait_recv()
        add_a(lax.rem(x + N - d, N))
        last_b[d].wait_recv()
        add_b(lax.rem(y + N - d, N))

    for copy in face_copies:
        copy.wait_recv()
    centre = model[0]
    height, width = centre.shape
    lane = lax.broadcasted_iota(jnp.int32, centre.shape, 1)
    zero = jnp.zeros_like(centre)
    before_t = jnp.where(tm > 0, faces[0], zero)
    after_t = jnp.where(tm < times - 1, faces[1], zero)
    before_s = jnp.where(sub > 0, faces[2], zero)
    after_s = jnp.where(sub < parts - 1, faces[3], zero)
    near = after_t + before_t
    near = near + jnp.concatenate([centre[1:], after_s[:1]], axis=0)
    near = near + jnp.concatenate([before_s[height - 1 :], centre[: height - 1]], axis=0)
    near = near + jnp.where(lane == width - 1, 0.0, pltpu.roll(centre, width - 1, 1))
    near = near + jnp.where(lane == 0, 0.0, pltpu.roll(centre, 1, 1))
    smooth = 6.0 * centre - near
    flat = jnp.sum(total[...], axis=0, keepdims=True)
    flat = (flat[:, :cells] + flat[:, cells : 2 * cells] + flat[:, 2 * cells :]) * scale
    for j in range(height):
        gradient_out[0, j : j + 1, :] = flat[:, j * width : (j + 1) * width] + smooth[j : j + 1]

    for copy in sent:
        copy.wait_send()


def body(field_grads, model, observed, data_weight):
    electrodes = field_grads.shape[2]
    columns = field_grads.shape[3]
    width = field_grads.shape[4]
    terms = 3 * columns * width
    own = observed.shape[1]
    half = electrodes // 2
    tile = N * own
    wide = half + LANES
    dma = pltpu.SemaphoreType.DMA
    vmem = pl.BlockSpec(memory_space=pltpu.VMEM)
    return pl.pallas_call(
        kernel,
        out_shape=(
            jax.ShapeDtypeStruct(observed.shape, F32),
            jax.ShapeDtypeStruct(model.shape, F32),
        ),
        in_specs=[pl.BlockSpec(memory_space=pltpu.HBM)] * 4,
        out_specs=(vmem, vmem),
        scratch_shapes=[
            pltpu.VMEM(model.shape, F32),
            pltpu.VMEM(observed.shape, F32),
            pltpu.VMEM(observed.shape, F32),
            pltpu.VMEM((3, electrodes, columns, width), BF16),
            pltpu.VMEM((electrodes, terms), BF16),
            pltpu.VMEM((electrodes, terms), BF16),
            pltpu.VMEM((N, N, own, half), F32),
            pltpu.VMEM((N, tile, wide), F32),
            pltpu.VMEM((N, N, own, half), BF16),
            pltpu.VMEM((N, tile, wide), BF16),
            pltpu.VMEM((3, N, own, half), BF16),
            pltpu.VMEM((3, tile, wide), BF16),
            pltpu.VMEM((N, own, half), F32),
            pltpu.VMEM((N, own, wide), F32),
            pltpu.VMEM((3, own, half), F32),
            pltpu.VMEM((3, own, wide), F32),
            pltpu.VMEM((2, own, wide), BF16),
            pltpu.VMEM((2, own, wide), BF16),
            pltpu.VMEM((N, N, own, half), BF16),
            pltpu.VMEM((N, N, own, wide), BF16),
            pltpu.VMEM((N, 4, own, LANES), F32),
            pltpu.VMEM((N, 4, own, LANES), F32),
            pltpu.VMEM((N, 4, own, LANES), F32),
            pltpu.VMEM((N, 4, own, LANES), F32),
            pltpu.VMEM((2, 2 * N + 1, own, LANES), F32),
            pltpu.VMEM((2, 2 * N + 1, own, LANES), BF16),
            pltpu.VMEM((2, 2 * N + 1, own, LANES), BF16),
            pltpu.VMEM((N, 2, own, LANES), F32),
            pltpu.VMEM((N, 2, own, LANES), F32),
            pltpu.VMEM((N, 2, own, LANES), F32),
            pltpu.VMEM((N, 2, own, LANES), F32),
            pltpu.VMEM((own, 2 * half + LANES), F32),
            pltpu.VMEM((8, terms), F32),
            pltpu.VMEM((4, columns, width), F32),
            dma((6,)),
            dma((48,)),
            dma((48,)),
        ],
        compiler_params=pltpu.CompilerParams(
            collective_id=0, has_side_effects=True, vmem_limit_bytes=64 * 1024 * 1024 - 65536
        ),
    )(field_grads, model, observed, data_weight)


def solution(mesh):
    return jax.shard_map(
        body,
        mesh=mesh,
        in_specs=(
            P("tm", None, None, "sub", None),
            P("tm", "sub", None),
            P("tm", "sub", None),
            P("tm", "sub", None),
        ),
        out_specs=(P("tm", "sub", None), P("tm", "sub", None)),
        check_vma=False,
    )
```

```python
import jax
import jax.numpy as jnp
from jax import lax
from jax.experimental import pallas as pl
from jax.experimental.pallas import tpu as pltpu
from jax.sharding import PartitionSpec as P

MESH = pl.DeviceIdType.MESH
F32 = jnp.float32
BF16 = jnp.bfloat16
N = 4
NZ = 2
LANES = 128
FAR_FIRST = (2, 1, 3)
NEAR_FIRST = (1, 3, 2)
STREAMS = (("b", (0, 1, 2)), ("a", (0, 1)), ("b", (3, 4)), ("a", (2, 3)))
BOXES = ("pairs", "send", "recv", "acc", "recv2", "z_send", "z_recv", "gather")


def kernel(
    fields,
    model_in,
    observed_in,
    weight_in,
    misfit_out,
    gradient_out,
    model,
    observed,
    weight,
    raw,
    grads,
    weighted,
    direct,
    data,
    data_y,
    data_t,
    data_x,
    data_u,
    data_b,
    data_z,
    post,
    post_y,
    post_t,
    post_x,
    potential,
    total,
    faces,
    load_sem,
    send_sem,
    recv_sem,
    *boxes,
):
    electrodes, terms = grads.shape
    half = electrodes // 2
    own = misfit_out.shape[1]
    tile = N * own
    cells = terms // 3
    parts = N * N * NZ
    tm = lax.axis_index("tm")
    sub = lax.axis_index("sub")
    times = lax.axis_size("tm")
    x = lax.rem(sub, N)
    y = lax.rem(sub // N, N)
    z = sub // (N * N)

    def at(zz, yy, xx):
        return {"sub": (zz * N + yy) * N + xx}

    def x_peer(d):
        return at(z, y, lax.rem(x + d, N))

    def y_peer(d):
        return at(z, lax.rem(y + d, N), x)

    z_peer = at(1 - z, y, x)
    beside = (
        {"tm": lax.rem(tm + 1, times)},
        {"tm": lax.rem(tm + times - 1, times)},
        {"sub": lax.rem(sub + 1, parts)},
        {"sub": lax.rem(sub + parts - 1, parts)},
    )
    sent = []

    def start(src, dst, peer):
        n = len(sent)
        copy = pltpu.make_async_remote_copy(
            src_ref=src,
            dst_ref=dst,
            send_sem=send_sem.at[n],
            recv_sem=recv_sem.at[n],
            device_id=peer,
            device_id_type=MESH,
        )
        sent.append(copy)
        copy.start()
        return copy

    loads = [pltpu.make_async_copy(fields.at[0, k], raw.at[k], load_sem.at[k]) for k in range(3)]
    inputs = [
        pltpu.make_async_copy(src, dst, load_sem.at[3 + n])
        for n, (src, dst) in enumerate(
            ((weight_in, weight), (observed_in, observed), (model_in, model))
        )
    ]
    for load in inputs + loads:
        load.start()

    barrier = pltpu.get_barrier_semaphore()
    peers = [x_peer(d) for d in FAR_FIRST] + [y_peer(d) for d in FAR_FIRST]
    peers += [z_peer] + list(beside)
    for peer in peers:
        pl.semaphore_signal(barrier, inc=1, device_id=peer, device_id_type=MESH)

    for load in inputs:
        load.wait()

    for n in range(2 * N):
        columns = slice(n * LANES, (n + 1) * LANES)
        e = weight[0, :, columns] * weight[0, :, columns]
        other = z if n < N else 1 - z
        direct[n % N, other] = e
        direct[n % N, 2 + other] = e * observed[0, :, columns]
    data[...] = direct[...].astype(BF16)

    def begin_y(box, box_y):
        copies = [
            start(box.at[lax.rem(y + d, N)], box_y.at[y], y_peer(d)) for d in FAR_FIRST
        ]
        box_y[y] = box[y]
        return copies

    def begin_x(copies, box_y, box_t, box_x):
        for copy in copies:
            copy.wait_recv()
        for q in range(box_y.shape[1]):
            square = jnp.concatenate([box_y[n, q].astype(F32) for n in range(N)], axis=0)
            turned = square.T
            for n in range(N):
                box_t[n, q] = turned[n * own : (n + 1) * own].astype(box_t.dtype)
        copies = [
            start(box_t.at[lax.rem(x + d, N)], box_x.at[x], x_peer(d)) for d in FAR_FIRST
        ]
        box_x[x] = box_t[x]
        return copies

    lane_block = lax.broadcasted_iota(jnp.int32, (own, LANES), 1) // own

    def mirrored(box_x, q, t):
        result = None
        for n in range(N):
            moved = box_x[n, q].astype(F32)
            if n != t:
                moved = pltpu.roll(moved, ((n - t) % N) * own, 1)
            result = moved if result is None else jnp.where(lane_block == n, moved, result)
        return result

    cell_row = jnp.concatenate([model[0, j : j + 1, :] for j in range(model.shape[1])], axis=1)

    def lay_out(k):
        loads[k].wait()
        columns = slice(k * cells, (k + 1) * cells)
        for n in range(4):
            rows = slice(n * 256, (n + 1) * 256)
            flat = raw[k, rows].reshape(256, cells)
            grads[rows, columns] = flat
            weighted[rows, columns] = (flat.astype(F32) * cell_row).astype(BF16)

    def product(rows, columns):
        return lax.dot_general(
            weighted[rows, :], grads[columns, :], (((1,), (1,)), ((), ())), preferred_element_type=F32
        )

    streams = []
    for n, (kind, tiles) in enumerate(STREAMS):
        box = dict(zip(BOXES, boxes[len(BOXES) * n : len(BOXES) * (n + 1)]))
        if kind == "a":
            box.update(outer=x, inner=y, outer_peer=x_peer, inner_peer=y_peer)
        else:
            box.update(outer=y, inner=x, outer_peer=y_peer, inner_peer=x_peer)
        box.update(tiles=tiles, first=N * (kind == "b") + tiles[0], width=len(tiles) * LANES)
        streams.append(box)

    lay_out(0)
    pl.semaphore_wait(barrier, len(peers))
    data_copies = begin_y(data, data_y)
    face_copies = [start(model.at[0], faces.at[n], peer) for n, peer in enumerate(beside)]
    lay_out(1)
    lay_out(2)

    def send_out(kind):
        for (which, _), box in zip(STREAMS, streams):
            if which == kind:
                box["one"] = [
                    start(box["send"].at[lax.rem(box["outer"] + d, N)], box["recv"].at[d - 1], box["outer_peer"](d))
                    for d in FAR_FIRST
                ]

    def keep_at(kind, outer, inner, place, piece):
        for (which, tiles), box in zip(STREAMS, streams):
            if which == kind and place in tiles:
                columns = slice((place - tiles[0]) * LANES, (place - tiles[0] + 1) * LANES)
                box["pairs"][outer, inner, :, columns] = piece
                box["send"][outer, inner, :, columns] = piece.astype(BF16)

    def keep(block, block_row, block_column, row, column, place):
        r = (row - block_row) * LANES
        c = (column - block_column) * LANES
        piece = block[r : r + LANES, c : c + LANES]
        for xx in range(N):
            keep_at("b", row, xx, place, piece[xx * own : (xx + 1) * own])

    for b in range(2):
        upper = product(slice(b * 256, (b + 1) * 256), slice(b * 256, half))
        lower = product(
            slice(half + b * 256, half + (b + 1) * 256), slice(half, half + (b + 1) * 256)
        )
        for row in (2 * b, 2 * b + 1):
            for column in range(N):
                if column >= row:
                    keep(upper, 2 * b, 2 * b, row, column, column)
                else:
                    keep(lower, 2 * b, 0, row, column, column)
            keep(lower, 2 * b, 0, row, row, N)
    send_out("b")
    data_copies = begin_x(data_copies, data_y, data_t, data_x)

    for b in range(2):
        block = product(slice(b * 256, (b + 1) * 256), slice(half, electrodes))
        for n in range(2):
            for xx in range(N):
                piece = block[n * tile + xx * own : n * tile + (xx + 1) * own]
                for t in range(N):
                    keep_at("a", xx, 2 * b + n, t, piece[:, t * LANES : (t + 1) * LANES])
    send_out("a")

    for copy in data_copies:
        copy.wait_recv()
    low = z == 0
    nil = jnp.zeros((own, LANES), F32)
    for v in range(2):
        for t in range(N):
            data_u[v, t] = jnp.where(low, direct[t, 2 * v + 1], mirrored(data_x, 2 * v + 1, t))
            plain = direct[t, 2 * v]
            both = plain + mirrored(data_x, 2 * v, t)
            inside = jnp.where(low, t > y, t < y)
            corner = jnp.logical_and(low, y == t)
            data_u[v, N + t] = jnp.where(inside, both, jnp.where(corner, plain, nil))
        data_u[v, 2 * N] = jnp.where(low, nil, direct[y, 2 * v])
    data_b[...] = data_u[...].astype(BF16)
    data_copy = start(data_b, data_z, z_peer)

    def arrived(copies, box):
        for copy in copies:
            copy.wait_recv()
        return box[0].astype(F32) + box[1].astype(F32) + box[2].astype(F32)

    for box in streams:
        box["acc"][...] = box["pairs"][box["outer"]] + arrived(box["one"], box["recv"])
        box["two"] = [
            start(box["acc"].at[lax.rem(box["inner"] + d, N)], box["recv2"].at[d - 1], box["inner_peer"](d))
            for d in FAR_FIRST
        ]
    for box in streams:
        summed = box["acc"][box["inner"]] + arrived(box["two"], box["recv2"])
        potential[:, box["first"] * LANES : box["first"] * LANES + box["width"]] = summed
        box["z_send"][...] = summed.astype(BF16)
        box["three"] = start(box["z_send"], box["z_recv"], z_peer)

    scale = 1.0 / jnp.sqrt(F32(cells * 3 * parts))
    data_copy.wait_recv()

    for box in streams:
        box["three"].wait_recv()
        block = box["gather"].at[box["outer"], box["inner"]]
        for n in range(len(box["tiles"])):
            t = box["first"] + n
            columns = slice(t * LANES, (t + 1) * LANES)
            inner = slice(n * LANES, (n + 1) * LANES)
            value = (potential[:, columns] + box["z_recv"][:, inner].astype(F32)) * scale
            potential[:, columns] = value
            factor = data_u[0, t] + data_z[0, t].astype(F32)
            residual = factor * value - (data_u[1, t] + data_z[1, t].astype(F32))
            block[:, inner] = residual.astype(BF16)
            if t < N:
                post[t, 1] = value
            elif t < 2 * N:
                post[t - N, 0] = value
        box["four"] = [start(block, block, box["inner_peer"](d)) for d in FAR_FIRST]
    post_copies = begin_y(post, post_y)
    for box in streams:
        for copy in box["four"]:
            copy.wait_recv()
        block = box["gather"].at[box["outer"]]
        box["five"] = {d: start(block, block, box["outer_peer"](d)) for d in FAR_FIRST}
    post_copies = begin_x(post_copies, post_y, post_t, post_x)

    total[...] = jnp.zeros_like(total)

    def collect(matrix, columns, rows):
        made = jnp.dot(matrix, grads[columns, :], preferred_element_type=F32)
        made = made * rows.astype(F32)
        total[...] += jnp.sum(made.reshape(tile // 8, 8, terms), axis=0)

    def at_rows(first, count):
        return pl.ds(pl.multiple_of(first, count), count)

    def gathered(kind, outer):
        return [
            box["gather"][outer].reshape(tile, box["width"])[:, n * LANES : (n + 1) * LANES]
            for (which, _), box in zip(STREAMS, streams)
            if which == kind
            for n in range(len(box["tiles"]))
        ]

    def add_a(xx):
        rows = jnp.concatenate([grads[at_rows(yy * tile + xx * own, own), :] for yy in range(N)], axis=0)
        matrix = jnp.concatenate(gathered("a", xx), axis=1)
        collect(matrix, slice(half, electrodes), rows)

    def add_b(yy):
        tiles = gathered("b", yy)
        none = jnp.zeros_like(tiles[0])
        upper = [jnp.where(yy <= t, tiles[t], none) for t in range(N)]
        lower = [
            jnp.where(yy > t, tiles[t], jnp.where(yy == t, tiles[N], none)) for t in range(N)
        ]
        collect(jnp.concatenate(upper, axis=1), slice(0, half), grads[at_rows(yy * tile, tile), :])
        collect(
            jnp.concatenate(lower, axis=1),
            slice(half, electrodes),
            grads[at_rows(half + yy * tile, tile), :],
        )

    add_a(x)
    add_b(y)

    for copy in post_copies:
        copy.wait_recv()
    for n in range(2 * N):
        columns = slice(n * LANES, (n + 1) * LANES)
        t = n % N
        between = potential[:, t * LANES : (t + 1) * LANES]
        within = potential[:, half + t * LANES : half + (t + 1) * LANES]
        corner = potential[:, 2 * half : 2 * half + LANES]
        turned = mirrored(post_x, 0, t)
        upper = jnp.where(y <= t, within, turned)
        lower = jnp.where(y > t, within, jnp.where(y == t, corner, turned))
        mine = jnp.where(low, upper, lower)
        others = jnp.where(low, between, mirrored(post_x, 1, t))
        here = low if n < N else z == 1
        value = jnp.where(here, mine, others)
        misfit_out[0, :, columns] = weight[0, :, columns] * (value - observed[0, :, columns])

    for d in NEAR_FIRST:
        for kind, add, mine in (("a", add_a, x), ("b", add_b, y)):
            for (which, _), box in zip(STREAMS, streams):
                if which == kind:
                    box["five"][d].wait_recv()
            add(lax.rem(mine + N - d, N))

    for copy in face_copies:
        copy.wait_recv()
    centre = model[0]
    height, width = centre.shape
    lane = lax.broadcasted_iota(jnp.int32, centre.shape, 1)
    zero = jnp.zeros_like(centre)
    before_t = jnp.where(tm > 0, faces[0], zero)
    after_t = jnp.where(tm < times - 1, faces[1], zero)
    before_s = jnp.where(sub > 0, faces[2], zero)
    after_s = jnp.where(sub < parts - 1, faces[3], zero)
    near = after_t + before_t
    near = near + jnp.concatenate([centre[1:], after_s[:1]], axis=0)
    near = near + jnp.concatenate([before_s[height - 1 :], centre[: height - 1]], axis=0)
    near = near + jnp.where(lane == width - 1, 0.0, pltpu.roll(centre, width - 1, 1))
    near = near + jnp.where(lane == 0, 0.0, pltpu.roll(centre, 1, 1))
    smooth = 6.0 * centre - near
    flat = jnp.sum(total[...], axis=0, keepdims=True)
    flat = (flat[:, :cells] + flat[:, cells : 2 * cells] + flat[:, 2 * cells :]) * scale
    for j in range(height):
        gradient_out[0, j : j + 1, :] = flat[:, j * width : (j + 1) * width] + smooth[j : j + 1]

    for copy in sent:
        copy.wait_send()


def body(field_grads, model, observed, data_weight):
    electrodes = field_grads.shape[2]
    columns = field_grads.shape[3]
    width = field_grads.shape[4]
    terms = 3 * columns * width
    own = observed.shape[1]
    half = electrodes // 2
    boxes = []
    for _, tiles in STREAMS:
        w = len(tiles) * LANES
        boxes += [
            pltpu.VMEM((N, N, own, w), F32),
            pltpu.VMEM((N, N, own, w), BF16),
            pltpu.VMEM((3, N, own, w), BF16),
            pltpu.VMEM((N, own, w), F32),
            pltpu.VMEM((3, own, w), F32),
            pltpu.VMEM((own, w), BF16),
            pltpu.VMEM((own, w), BF16),
            pltpu.VMEM((N, N, own, w), BF16),
        ]
    dma = pltpu.SemaphoreType.DMA
    vmem = pl.BlockSpec(memory_space=pltpu.VMEM)
    return pl.pallas_call(
        kernel,
        out_shape=(
            jax.ShapeDtypeStruct(observed.shape, F32),
            jax.ShapeDtypeStruct(model.shape, F32),
        ),
        in_specs=[pl.BlockSpec(memory_space=pltpu.HBM)] * 4,
        out_specs=(vmem, vmem),
        scratch_shapes=[
            pltpu.VMEM(model.shape, F32),
            pltpu.VMEM(observed.shape, F32),
            pltpu.VMEM(observed.shape, F32),
            pltpu.VMEM((3, electrodes, columns, width), BF16),
            pltpu.VMEM((electrodes, terms), BF16),
            pltpu.VMEM((electrodes, terms), BF16),
            pltpu.VMEM((N, 4, own, LANES), F32),
            pltpu.VMEM((N, 4, own, LANES), BF16),
            pltpu.VMEM((N, 4, own, LANES), BF16),
            pltpu.VMEM((N, 4, own, LANES), BF16),
            pltpu.VMEM((N, 4, own, LANES), BF16),
            pltpu.VMEM((2, 2 * N + 1, own, LANES), F32),
            pltpu.VMEM((2, 2 * N + 1, own, LANES), BF16),
            pltpu.VMEM((2, 2 * N + 1, own, LANES), BF16),
            pltpu.VMEM((N, 2, own, LANES), F32),
            pltpu.VMEM((N, 2, own, LANES), F32),
            pltpu.VMEM((N, 2, own, LANES), F32),
            pltpu.VMEM((N, 2, own, LANES), F32),
            pltpu.VMEM((own, 2 * half + LANES), F32),
            pltpu.VMEM((8, terms), F32),
            pltpu.VMEM((4, columns, width), F32),
            dma((6,)),
            dma((72,)),
            dma((72,)),
        ]
        + boxes,
        compiler_params=pltpu.CompilerParams(
            collective_id=0, has_side_effects=True, vmem_limit_bytes=64 * 1024 * 1024 - 65536
        ),
    )(field_grads, model, observed, data_weight)


def solution(mesh):
    return jax.shard_map(
        body,
        mesh=mesh,
        in_specs=(
            P("tm", None, None, "sub", None),
            P("tm", "sub", None),
            P("tm", "sub", None),
            P("tm", "sub", None),
        ),
        out_specs=(P("tm", "sub", None), P("tm", "sub", None)),
        check_vma=False,
    )
```

```python
import jax
import jax.numpy as jnp
from jax import lax
from jax.experimental import pallas as pl
from jax.experimental.pallas import tpu as pltpu
from jax.sharding import PartitionSpec as P

MESH = pl.DeviceIdType.MESH
F32 = jnp.float32
BF16 = jnp.bfloat16
N = 4
NZ = 2
LANES = 128
FAR_FIRST = (2, 1, 3)
STREAMS = (("b", (0, 1)), ("a", (0, 1)), ("b", (2, 3, 4)), ("a", (2, 3)))
BOXES = ("pairs", "send", "recv", "acc", "recv2", "z_send", "z_recv", "gather")


class Copy:
    def __init__(self, copy, sends, receives):
        self.copy = copy
        self.sends = sends
        self.receives = receives

    def start(self):
        when(self.sends, self.copy.start)

    def wait_send(self):
        when(self.sends, self.copy.wait_send)

    def wait_recv(self):
        when(self.receives, self.copy.wait_recv)


def when(condition, action):
    if condition is None:
        action()
    else:

        @pl.when(condition)
        def _():
            action()


def kernel(
    fields,
    model_in,
    observed_in,
    weight_in,
    misfit_out,
    gradient_out,
    model,
    observed,
    weight,
    raw,
    grads,
    weighted,
    direct,
    data,
    data_y,
    data_t,
    data_x,
    data_u,
    data_b,
    data_z,
    post,
    post_y,
    post_t,
    post_x,
    potential,
    total,
    faces,
    load_sem,
    send_sem,
    recv_sem,
    plane_sem,
    *boxes,
):
    electrodes, terms = grads.shape
    half = electrodes // 2
    own = misfit_out.shape[1]
    tile = N * own
    cells = terms // 3
    parts = N * N * NZ
    tm = lax.axis_index("tm")
    sub = lax.axis_index("sub")
    times = lax.axis_size("tm")
    x = lax.rem(sub, N)
    y = lax.rem(sub // N, N)
    z = sub // (N * N)

    def at(zz, yy, xx):
        return {"sub": (zz * N + yy) * N + xx}

    def x_peer(d):
        return at(z, y, lax.rem(x + d, N))

    def y_peer(d):
        return at(z, lax.rem(y + d, N), x)

    z_peer = at(1 - z, y, x)
    beside = (
        ({"tm": lax.rem(tm + 1, times)}, tm < times - 1, tm > 0),
        ({"tm": lax.rem(tm + times - 1, times)}, tm > 0, tm < times - 1),
        ({"sub": lax.rem(sub + 1, parts)}, sub < parts - 1, sub > 0),
        ({"sub": lax.rem(sub + parts - 1, parts)}, sub > 0, sub < parts - 1),
    )
    sent = []

    def start(src, dst, peer, sends=None, receives=None):
        n = len(sent)
        copy = Copy(
            pltpu.make_async_remote_copy(
                src_ref=src,
                dst_ref=dst,
                send_sem=send_sem.at[n],
                recv_sem=recv_sem.at[n],
                device_id=peer,
                device_id_type=MESH,
            ),
            sends,
            receives,
        )
        sent.append(copy)
        copy.start()
        return copy

    loads = [pltpu.make_async_copy(fields.at[0, k], raw.at[k], load_sem.at[k]) for k in range(3)]
    inputs = [
        pltpu.make_async_copy(src, dst, load_sem.at[3 + n])
        for n, (src, dst) in enumerate(
            ((weight_in, weight), (observed_in, observed), (model_in, model))
        )
    ]
    for load in inputs + loads:
        load.start()

    barrier = pltpu.get_barrier_semaphore()
    plane = [x_peer(d) for d in FAR_FIRST] + [y_peer(d) for d in FAR_FIRST]

    def greet(peer, condition=None):
        when(
            condition,
            lambda: pl.semaphore_signal(barrier, inc=1, device_id=peer, device_id_type=MESH),
        )

    greet(z_peer, z == 0)
    for peer in plane:
        greet(peer)
    for peer, condition, _ in beside[:2]:
        greet(peer, condition)
    greetings = len(plane) + z + jnp.where(tm > 0, 1, 0) + jnp.where(tm < times - 1, 1, 0)

    for load in inputs:
        load.wait()

    for n in range(2 * N):
        columns = slice(n * LANES, (n + 1) * LANES)
        e = weight[0, :, columns] * weight[0, :, columns]
        other = z if n < N else 1 - z
        direct[n % N, other] = e
        direct[n % N, 2 + other] = e * observed[0, :, columns]
    data[...] = direct[...].astype(BF16)

    def begin_y(box, box_y, conditions):
        copies = exchange(box, box_y, y, y_peer, conditions)
        box_y[y] = box[y]
        return copies

    def begin_x(copies, box_y, box_t, box_x, conditions):
        for copy in copies:
            copy.wait_recv()
        for q in range(box_y.shape[1]):
            square = jnp.concatenate([box_y[n, q].astype(F32) for n in range(N)], axis=0)
            turned = square.T
            for n in range(N):
                box_t[n, q] = turned[n * own : (n + 1) * own].astype(box_t.dtype)
        copies = exchange(box_t, box_x, x, x_peer, conditions)
        box_x[x] = box_t[x]
        return copies

    def exchange(src, dst, mine, peer_of, conditions):
        if conditions is None:
            return [start(src.at[lax.rem(mine + d, N)], dst.at[mine], peer_of(d)) for d in FAR_FIRST]
        return [
            start(src.at[lax.rem(mine + d, N), q], dst.at[mine, q], peer_of(d), condition, condition)
            for q, condition in enumerate(conditions)
            for d in FAR_FIRST
        ]

    lane_block = lax.broadcasted_iota(jnp.int32, (own, LANES), 1) // own

    def mirrored(box_x, q, t):
        result = None
        for n in range(N):
            moved = box_x[n, q].astype(F32)
            if n != t:
                moved = pltpu.roll(moved, ((n - t) % N) * own, 1)
            result = moved if result is None else jnp.where(lane_block == n, moved, result)
        return result

    cell_row = jnp.concatenate([model[0, j : j + 1, :] for j in range(model.shape[1])], axis=1)

    def lay_out(k):
        loads[k].wait()
        columns = slice(k * cells, (k + 1) * cells)
        for n in range(4):
            rows = slice(n * 256, (n + 1) * 256)
            flat = raw[k, rows].reshape(256, cells)
            grads[rows, columns] = flat
            weighted[rows, columns] = (flat.astype(F32) * cell_row).astype(BF16)

    def product(rows, columns):
        return lax.dot_general(
            weighted[rows, :], grads[columns, :], (((1,), (1,)), ((), ())), preferred_element_type=F32
        )

    streams = []
    for n, (kind, tiles) in enumerate(STREAMS):
        box = dict(zip(BOXES, boxes[len(BOXES) * n : len(BOXES) * (n + 1)]))
        if kind == "a":
            box.update(outer=x, inner=y, outer_peer=x_peer, inner_peer=y_peer)
        else:
            box.update(outer=y, inner=x, outer_peer=y_peer, inner_peer=x_peer)
        box.update(tiles=tiles, first=N * (kind == "b") + tiles[0], width=len(tiles) * LANES)
        streams.append(box)

    lay_out(0)
    pl.semaphore_wait(barrier, greetings)
    when(
        z == 1,
        lambda: pl.semaphore_signal(plane_sem, inc=1, device_id=z_peer, device_id_type=MESH),
    )
    data_copies = begin_y(data, data_y, None)

    def send_faces(first):
        return [
            start(model.at[0], faces.at[first + n], *beside[first + n]) for n in range(2)
        ]

    face_copies = send_faces(0)
    lay_out(1)
    lay_out(2)

    def send_out(kind):
        for (which, _), box in zip(STREAMS, streams):
            if which == kind:
                box["one"] = [
                    start(box["send"].at[lax.rem(box["outer"] + d, N)], box["recv"].at[d - 1], box["outer_peer"](d))
                    for d in FAR_FIRST
                ]

    def keep_at(kind, outer, inner, place, piece):
        for (which, tiles), box in zip(STREAMS, streams):
            if which == kind and place in tiles:
                columns = slice((place - tiles[0]) * LANES, (place - tiles[0] + 1) * LANES)
                box["pairs"][outer, inner, :, columns] = piece
                box["send"][outer, inner, :, columns] = piece.astype(BF16)

    def keep(block, block_row, block_column, row, column, place):
        r = (row - block_row) * LANES
        c = (column - block_column) * LANES
        piece = block[r : r + LANES, c : c + LANES]
        for xx in range(N):
            keep_at("b", row, xx, place, piece[xx * own : (xx + 1) * own])

    for b in range(2):
        upper = product(slice(b * 256, (b + 1) * 256), slice(b * 256, half))
        lower = product(
            slice(half + b * 256, half + (b + 1) * 256), slice(half, half + (b + 1) * 256)
        )
        for row in (2 * b, 2 * b + 1):
            for column in range(N):
                if column >= row:
                    keep(upper, 2 * b, 2 * b, row, column, column)
                else:
                    keep(lower, 2 * b, 0, row, column, column)
            keep(lower, 2 * b, 0, row, row, N)
    send_out("b")
    data_copies = begin_x(data_copies, data_y, data_t, data_x, None)

    for b in range(2):
        block = product(slice(b * 256, (b + 1) * 256), slice(half, electrodes))
        for n in range(2):
            for xx in range(N):
                piece = block[n * tile + xx * own : n * tile + (xx + 1) * own]
                for t in range(N):
                    keep_at("a", xx, 2 * b + n, t, piece[:, t * LANES : (t + 1) * LANES])
    send_out("a")

    for copy in data_copies:
        copy.wait_recv()
    low = z == 0
    nil = jnp.zeros((own, LANES), F32)
    for v in range(2):
        for t in range(N):
            data_u[v, t] = jnp.where(low, direct[t, 2 * v + 1], mirrored(data_x, 2 * v + 1, t))
            plain = direct[t, 2 * v]
            both = plain + mirrored(data_x, 2 * v, t)
            inside = jnp.where(low, t > y, t < y)
            corner = jnp.logical_and(low, y == t)
            data_u[v, N + t] = jnp.where(inside, both, jnp.where(corner, plain, nil))
        data_u[v, 2 * N] = jnp.where(low, nil, direct[y, 2 * v])
    data_b[...] = data_u[...].astype(BF16)
    when(z == 0, lambda: pl.semaphore_wait(plane_sem, 1))
    data_copy = start(data_b, data_z, z_peer)

    def arrived(copies, box):
        for copy in copies:
            copy.wait_recv()
        return box[0].astype(F32) + box[1].astype(F32) + box[2].astype(F32)

    for box in streams:
        box["acc"][...] = box["pairs"][box["outer"]] + arrived(box["one"], box["recv"])
        box["two"] = [
            start(box["acc"].at[lax.rem(box["inner"] + d, N)], box["recv2"].at[d - 1], box["inner_peer"](d))
            for d in FAR_FIRST
        ]
    for box in streams:
        summed = box["acc"][box["inner"]] + arrived(box["two"], box["recv2"])
        potential[:, box["first"] * LANES : box["first"] * LANES + box["width"]] = summed
        box["z_send"][...] = summed.astype(BF16)
        box["three"] = start(box["z_send"], box["z_recv"], z_peer)

    scale = 1.0 / jnp.sqrt(F32(cells * 3 * parts))
    data_copy.wait_recv()

    for box in streams:
        box["three"].wait_recv()
        block = box["gather"].at[box["outer"], box["inner"]]
        for n in range(len(box["tiles"])):
            t = box["first"] + n
            columns = slice(t * LANES, (t + 1) * LANES)
            inner = slice(n * LANES, (n + 1) * LANES)
            value = (potential[:, columns] + box["z_recv"][:, inner].astype(F32)) * scale
            potential[:, columns] = value
            factor = data_u[0, t] + data_z[0, t].astype(F32)
            residual = factor * value - (data_u[1, t] + data_z[1, t].astype(F32))
            block[:, inner] = residual.astype(BF16)
            if t < N:
                post[t, 1] = value
            elif t < 2 * N:
                post[t - N, 0] = value
        box["four"] = [start(block, block, box["inner_peer"](d)) for d in FAR_FIRST]
    face_copies += send_faces(2)
    post_copies = begin_y(post, post_y, (None, z == 1))
    for box in streams:
        for copy in box["four"]:
            copy.wait_recv()
        block = box["gather"].at[box["outer"]]
        box["five"] = [start(block, block, box["outer_peer"](d)) for d in FAR_FIRST]
    post_copies = begin_x(post_copies, post_y, post_t, post_x, (None, z == 1))

    total[...] = jnp.zeros_like(total)

    def collect(matrix, columns, pieces):
        count = matrix.shape[0]
        for k in range(3):
            span = slice(k * cells, (k + 1) * cells)
            made = jnp.dot(matrix, grads[columns, span], preferred_element_type=F32)
            rows = [grads[piece, span] for piece in pieces]
            rows = rows[0] if len(rows) == 1 else jnp.concatenate(rows, axis=0)
            made = made * rows.astype(F32)
            total[:, span] += jnp.sum(made.reshape(count // 8, 8, cells), axis=0)

    none = jnp.zeros((tile, LANES), BF16)

    def stack(rows):
        return jnp.concatenate([jnp.concatenate(row, axis=1) for row in rows], axis=0)

    def add_a(box):
        first = half + box["tiles"][0] * LANES
        pieces = [
            slice(yy * tile + xx * own, yy * tile + (xx + 1) * own)
            for xx in range(N)
            for yy in range(N)
        ]
        matrix = box["gather"][...].reshape(half, box["width"])
        collect(matrix, slice(first, first + box["width"]), pieces)

    def tiles_of(box):
        found = {}
        for yy in range(N):
            rows = box["gather"][yy].reshape(tile, box["width"])
            for n, t in enumerate(box["tiles"]):
                found[yy, t] = rows[:, n * LANES : (n + 1) * LANES]
        return found

    def add_b(box):
        f = tiles_of(box)
        if box["tiles"][0] == 0:
            collect(stack([[f[0, 0], f[0, 1]], [none, f[1, 1]]]), slice(0, 256), [slice(0, 256)])
            collect(
                stack([[f[1, 0], none], [f[2, 0], f[2, 1]], [f[3, 0], f[3, 1]]]),
                slice(half, half + 256),
                [slice(half + tile, electrodes)],
            )
        else:
            collect(
                stack([[f[0, 2], f[0, 3]], [f[1, 2], f[1, 3]], [f[2, 2], f[2, 3]], [none, f[3, 3]]]),
                slice(256, half),
                [slice(0, half)],
            )
            collect(
                stack([[f[0, N], none], [none, f[1, N]]]),
                slice(half, half + 256),
                [slice(half, half + 256)],
            )
            collect(
                stack([[f[2, N], none], [f[3, 2], f[3, N]]]),
                slice(half + 256, electrodes),
                [slice(half + 256, electrodes)],
            )

    def finish_misfit():
        for copy in post_copies:
            copy.wait_recv()
        for n in range(2 * N):
            columns = slice(n * LANES, (n + 1) * LANES)
            t = n % N
            between = potential[:, t * LANES : (t + 1) * LANES]
            within = potential[:, half + t * LANES : half + (t + 1) * LANES]
            corner = potential[:, 2 * half : 2 * half + LANES]
            turned = mirrored(post_x, 0, t)
            upper = jnp.where(y <= t, within, turned)
            lower = jnp.where(y > t, within, jnp.where(y == t, corner, turned))
            mine = jnp.where(low, upper, lower)
            others = jnp.where(low, between, mirrored(post_x, 1, t))
            here = low if n < N else z == 1
            value = jnp.where(here, mine, others)
            misfit_out[0, :, columns] = weight[0, :, columns] * (value - observed[0, :, columns])

    for n, ((kind, _), box) in enumerate(zip(STREAMS, streams)):
        for copy in box["five"]:
            copy.wait_recv()
        if kind == "a":
            add_a(box)
        else:
            add_b(box)
        if n == 1:
            finish_misfit()

    for copy in face_copies:
        copy.wait_recv()
    centre = model[0]
    height, width = centre.shape
    lane = lax.broadcasted_iota(jnp.int32, centre.shape, 1)
    zero = jnp.zeros_like(centre)
    before_t = jnp.where(tm > 0, faces[0], zero)
    after_t = jnp.where(tm < times - 1, faces[1], zero)
    before_s = jnp.where(sub > 0, faces[2], zero)
    after_s = jnp.where(sub < parts - 1, faces[3], zero)
    near = after_t + before_t
    near = near + jnp.concatenate([centre[1:], after_s[:1]], axis=0)
    near = near + jnp.concatenate([before_s[height - 1 :], centre[: height - 1]], axis=0)
    near = near + jnp.where(lane == width - 1, 0.0, pltpu.roll(centre, width - 1, 1))
    near = near + jnp.where(lane == 0, 0.0, pltpu.roll(centre, 1, 1))
    smooth = 6.0 * centre - near
    flat = jnp.sum(total[...], axis=0, keepdims=True)
    flat = (flat[:, :cells] + flat[:, cells : 2 * cells] + flat[:, 2 * cells :]) * scale
    for j in range(height):
        gradient_out[0, j : j + 1, :] = flat[:, j * width : (j + 1) * width] + smooth[j : j + 1]

    for copy in sent:
        copy.wait_send()


def body(field_grads, model, observed, data_weight):
    electrodes = field_grads.shape[2]
    columns = field_grads.shape[3]
    width = field_grads.shape[4]
    terms = 3 * columns * width
    own = observed.shape[1]
    half = electrodes // 2
    boxes = []
    for _, tiles in STREAMS:
        w = len(tiles) * LANES
        boxes += [
            pltpu.VMEM((N, N, own, w), F32),
            pltpu.VMEM((N, N, own, w), BF16),
            pltpu.VMEM((3, N, own, w), BF16),
            pltpu.VMEM((N, own, w), F32),
            pltpu.VMEM((3, own, w), F32),
            pltpu.VMEM((own, w), BF16),
            pltpu.VMEM((own, w), BF16),
            pltpu.VMEM((N, N, own, w), BF16),
        ]
    dma = pltpu.SemaphoreType.DMA
    vmem = pl.BlockSpec(memory_space=pltpu.VMEM)
    return pl.pallas_call(
        kernel,
        out_shape=(
            jax.ShapeDtypeStruct(observed.shape, F32),
            jax.ShapeDtypeStruct(model.shape, F32),
        ),
        in_specs=[pl.BlockSpec(memory_space=pltpu.HBM)] * 4,
        out_specs=(vmem, vmem),
        scratch_shapes=[
            pltpu.VMEM(model.shape, F32),
            pltpu.VMEM(observed.shape, F32),
            pltpu.VMEM(observed.shape, F32),
            pltpu.VMEM((3, electrodes, columns, width), BF16),
            pltpu.VMEM((electrodes, terms), BF16),
            pltpu.VMEM((electrodes, terms), BF16),
            pltpu.VMEM((N, 4, own, LANES), F32),
            pltpu.VMEM((N, 4, own, LANES), BF16),
            pltpu.VMEM((N, 4, own, LANES), BF16),
            pltpu.VMEM((N, 4, own, LANES), BF16),
            pltpu.VMEM((N, 4, own, LANES), BF16),
            pltpu.VMEM((2, 2 * N + 1, own, LANES), F32),
            pltpu.VMEM((2, 2 * N + 1, own, LANES), BF16),
            pltpu.VMEM((2, 2 * N + 1, own, LANES), BF16),
            pltpu.VMEM((N, 2, own, LANES), F32),
            pltpu.VMEM((N, 2, own, LANES), F32),
            pltpu.VMEM((N, 2, own, LANES), F32),
            pltpu.VMEM((N, 2, own, LANES), F32),
            pltpu.VMEM((own, 2 * half + LANES), F32),
            pltpu.VMEM((8, terms), F32),
            pltpu.VMEM((4, columns, width), F32),
            dma((6,)),
            dma((80,)),
            dma((80,)),
            pltpu.SemaphoreType.REGULAR,
        ]
        + boxes,
        compiler_params=pltpu.CompilerParams(
            collective_id=0, has_side_effects=True, vmem_limit_bytes=64 * 1024 * 1024 - 65536
        ),
    )(field_grads, model, observed, data_weight)


def solution(mesh):
    return jax.shard_map(
        body,
        mesh=mesh,
        in_specs=(
            P("tm", None, None, "sub", None),
            P("tm", "sub", None),
            P("tm", "sub", None),
            P("tm", "sub", None),
        ),
        out_specs=(P("tm", "sub", None), P("tm", "sub", None)),
        check_vma=False,
    )
```

```python
import jax
import jax.numpy as jnp
from jax import lax
from jax.experimental import pallas as pl
from jax.experimental.pallas import tpu as pltpu
from jax.sharding import PartitionSpec as P

MESH = pl.DeviceIdType.MESH
F32 = jnp.float32
BF16 = jnp.bfloat16
N = 4
NZ = 2
LANES = 128
FAR_FIRST = (2, 1, 3)
STREAMS = (("b", (0, 1)), ("a", (0, 1)), ("b", (2, 3, 4)), ("a", (2, 3)))
BOXES = ("pairs", "send", "recv", "acc", "recv2", "z_send", "z_recv", "gather")


class Copy:
    def __init__(self, copy, sends, receives):
        self.copy = copy
        self.sends = sends
        self.receives = receives

    def start(self):
        when(self.sends, self.copy.start)

    def wait_send(self):
        when(self.sends, self.copy.wait_send)

    def wait_recv(self):
        when(self.receives, self.copy.wait_recv)


def when(condition, action):
    if condition is None:
        action()
    else:

        @pl.when(condition)
        def _():
            action()


def kernel(
    fields,
    model_in,
    observed_in,
    weight_in,
    misfit_out,
    gradient_out,
    model,
    observed,
    weight,
    raw,
    grads,
    weighted,
    direct,
    data,
    data_y,
    data_t,
    data_x,
    data_u,
    data_b,
    data_z,
    post,
    post_y,
    post_t,
    post_x,
    potential,
    total,
    faces,
    load_sem,
    send_sem,
    recv_sem,
    plane_sem,
    *boxes,
):
    electrodes, terms = grads.shape
    half = electrodes // 2
    own = misfit_out.shape[1]
    tile = N * own
    cells = terms // 3
    parts = N * N * NZ
    tm = lax.axis_index("tm")
    sub = lax.axis_index("sub")
    times = lax.axis_size("tm")
    x = lax.rem(sub, N)
    y = lax.rem(sub // N, N)
    z = sub // (N * N)

    def at(zz, yy, xx):
        return {"sub": (zz * N + yy) * N + xx}

    def x_peer(d):
        return at(z, y, lax.rem(x + d, N))

    def y_peer(d):
        return at(z, lax.rem(y + d, N), x)

    z_peer = at(1 - z, y, x)
    beside = (
        ({"tm": lax.rem(tm + 1, times)}, tm < times - 1, tm > 0),
        ({"tm": lax.rem(tm + times - 1, times)}, tm > 0, tm < times - 1),
        ({"sub": lax.rem(sub + 1, parts)}, sub < parts - 1, sub > 0),
        ({"sub": lax.rem(sub + parts - 1, parts)}, sub > 0, sub < parts - 1),
    )
    sent = []

    def start(src, dst, peer, sends=None, receives=None):
        n = len(sent)
        copy = Copy(
            pltpu.make_async_remote_copy(
                src_ref=src,
                dst_ref=dst,
                send_sem=send_sem.at[n],
                recv_sem=recv_sem.at[n],
                device_id=peer,
                device_id_type=MESH,
            ),
            sends,
            receives,
        )
        sent.append(copy)
        copy.start()
        return copy

    loads = [pltpu.make_async_copy(fields.at[0, k], raw.at[k], load_sem.at[k]) for k in range(3)]
    inputs = [
        pltpu.make_async_copy(src, dst, load_sem.at[3 + n])
        for n, (src, dst) in enumerate(
            ((weight_in, weight), (observed_in, observed), (model_in, model))
        )
    ]
    for load in inputs + loads:
        load.start()

    barrier = pltpu.get_barrier_semaphore()
    plane = [x_peer(d) for d in FAR_FIRST] + [y_peer(d) for d in FAR_FIRST]

    def greet(peer, condition=None):
        when(
            condition,
            lambda: pl.semaphore_signal(barrier, inc=1, device_id=peer, device_id_type=MESH),
        )

    greet(z_peer, z == 0)
    for peer in plane:
        greet(peer)
    for peer, condition, _ in beside[:2]:
        greet(peer, condition)
    greetings = len(plane) + z + jnp.where(tm > 0, 1, 0) + jnp.where(tm < times - 1, 1, 0)

    for load in inputs:
        load.wait()

    for n in range(2 * N):
        columns = slice(n * LANES, (n + 1) * LANES)
        e = weight[0, :, columns] * weight[0, :, columns]
        other = z if n < N else 1 - z
        direct[n % N, other] = e
        direct[n % N, 2 + other] = e * observed[0, :, columns]
    data[...] = direct[...].astype(BF16)

    def begin_y(box, box_y, conditions):
        copies = exchange(box, box_y, y, y_peer, conditions)
        box_y[y] = box[y]
        return copies

    def begin_x(copies, box_y, box_t, box_x, conditions):
        for copy in copies:
            copy.wait_recv()
        for q in range(box_y.shape[1]):
            square = jnp.concatenate([box_y[n, q].astype(F32) for n in range(N)], axis=0)
            turned = square.T
            for n in range(N):
                box_t[n, q] = turned[n * own : (n + 1) * own].astype(box_t.dtype)
        copies = exchange(box_t, box_x, x, x_peer, conditions)
        box_x[x] = box_t[x]
        return copies

    def exchange(src, dst, mine, peer_of, conditions):
        if conditions is None:
            return [start(src.at[lax.rem(mine + d, N)], dst.at[mine], peer_of(d)) for d in FAR_FIRST]
        return [
            start(src.at[lax.rem(mine + d, N), q], dst.at[mine, q], peer_of(d), condition, condition)
            for q, condition in enumerate(conditions)
            for d in FAR_FIRST
        ]

    lane_block = lax.broadcasted_iota(jnp.int32, (own, LANES), 1) // own

    def mirrored(box_x, q, t):
        result = None
        for n in range(N):
            moved = box_x[n, q].astype(F32)
            if n != t:
                moved = pltpu.roll(moved, ((n - t) % N) * own, 1)
            result = moved if result is None else jnp.where(lane_block == n, moved, result)
        return result

    cell_row = jnp.concatenate([model[0, j : j + 1, :] for j in range(model.shape[1])], axis=1)

    def lay_out(k):
        loads[k].wait()
        columns = slice(k * cells, (k + 1) * cells)
        for n in range(4):
            rows = slice(n * 256, (n + 1) * 256)
            flat = raw[k, rows].reshape(256, cells)
            grads[rows, columns] = flat
            weighted[rows, columns] = (flat.astype(F32) * cell_row).astype(BF16)

    def product(rows, columns):
        return lax.dot_general(
            weighted[rows, :], grads[columns, :], (((1,), (1,)), ((), ())), preferred_element_type=F32
        )

    streams = []
    for n, (kind, tiles) in enumerate(STREAMS):
        box = dict(zip(BOXES, boxes[len(BOXES) * n : len(BOXES) * (n + 1)]))
        if kind == "a":
            box.update(outer=x, inner=y, outer_peer=x_peer, inner_peer=y_peer)
        else:
            box.update(outer=y, inner=x, outer_peer=y_peer, inner_peer=x_peer)
        box.update(tiles=tiles, first=N * (kind == "b") + tiles[0], width=len(tiles) * LANES)
        streams.append(box)

    lay_out(0)
    pl.semaphore_wait(barrier, greetings)
    when(
        z == 1,
        lambda: pl.semaphore_signal(plane_sem, inc=1, device_id=z_peer, device_id_type=MESH),
    )
    data_copies = begin_y(data, data_y, None)

    def send_faces(first):
        return [
            start(model.at[0], faces.at[first + n], *beside[first + n]) for n in range(2)
        ]

    face_copies = send_faces(0)
    lay_out(1)
    lay_out(2)

    def send_out(kind):
        for (which, _), box in zip(STREAMS, streams):
            if which == kind:
                box["one"] = [
                    start(box["send"].at[lax.rem(box["outer"] + d, N)], box["recv"].at[d - 1], box["outer_peer"](d))
                    for d in FAR_FIRST
                ]

    def keep_at(kind, outer, inner, place, piece):
        for (which, tiles), box in zip(STREAMS, streams):
            if which == kind and place in tiles:
                columns = slice((place - tiles[0]) * LANES, (place - tiles[0] + 1) * LANES)
                box["pairs"][outer, inner, :, columns] = piece
                box["send"][outer, inner, :, columns] = piece.astype(BF16)

    def keep(block, block_row, block_column, row, column, place):
        r = (row - block_row) * LANES
        c = (column - block_column) * LANES
        piece = block[r : r + LANES, c : c + LANES]
        for xx in range(N):
            keep_at("b", row, xx, place, piece[xx * own : (xx + 1) * own])

    for b in range(2):
        upper = product(slice(b * 256, (b + 1) * 256), slice(b * 256, half))
        lower = product(
            slice(half + b * 256, half + (b + 1) * 256), slice(half, half + (b + 1) * 256)
        )
        for row in (2 * b, 2 * b + 1):
            for column in range(N):
                if column >= row:
                    keep(upper, 2 * b, 2 * b, row, column, column)
                else:
                    keep(lower, 2 * b, 0, row, column, column)
            keep(lower, 2 * b, 0, row, row, N)
    send_out("b")
    data_copies = begin_x(data_copies, data_y, data_t, data_x, None)

    for b in range(2):
        block = product(slice(b * 256, (b + 1) * 256), slice(half, electrodes))
        for n in range(2):
            for xx in range(N):
                piece = block[n * tile + xx * own : n * tile + (xx + 1) * own]
                for t in range(N):
                    keep_at("a", xx, 2 * b + n, t, piece[:, t * LANES : (t + 1) * LANES])
    send_out("a")

    for copy in data_copies:
        copy.wait_recv()
    low = z == 0
    nil = jnp.zeros((own, LANES), F32)
    for v in range(2):
        for t in range(N):
            data_u[v, t] = jnp.where(low, direct[t, 2 * v + 1], mirrored(data_x, 2 * v + 1, t))
            plain = direct[t, 2 * v]
            both = plain + mirrored(data_x, 2 * v, t)
            inside = jnp.where(low, t > y, t < y)
            corner = jnp.logical_and(low, y == t)
            data_u[v, N + t] = jnp.where(inside, both, jnp.where(corner, plain, nil))
        data_u[v, 2 * N] = jnp.where(low, nil, direct[y, 2 * v])
    data_b[...] = data_u[...].astype(BF16)
    when(z == 0, lambda: pl.semaphore_wait(plane_sem, 1))
    data_copy = start(data_b, data_z, z_peer)

    def arrived(copies, box):
        for copy in copies:
            copy.wait_recv()
        return box[0].astype(F32) + box[1].astype(F32) + box[2].astype(F32)

    for box in streams:
        box["acc"][...] = box["pairs"][box["outer"]] + arrived(box["one"], box["recv"])
        box["two"] = [
            start(box["acc"].at[lax.rem(box["inner"] + d, N)], box["recv2"].at[d - 1], box["inner_peer"](d))
            for d in FAR_FIRST
        ]
    for box in streams:
        summed = box["acc"][box["inner"]] + arrived(box["two"], box["recv2"])
        potential[:, box["first"] * LANES : box["first"] * LANES + box["width"]] = summed
        box["z_send"][...] = summed.astype(BF16)
        box["three"] = start(box["z_send"], box["z_recv"], z_peer)

    scale = 1.0 / jnp.sqrt(F32(cells * 3 * parts))
    data_copy.wait_recv()

    for box in streams:
        box["three"].wait_recv()
        block = box["gather"].at[box["outer"], box["inner"]]
        for n in range(len(box["tiles"])):
            t = box["first"] + n
            columns = slice(t * LANES, (t + 1) * LANES)
            inner = slice(n * LANES, (n + 1) * LANES)
            value = (potential[:, columns] + box["z_recv"][:, inner].astype(F32)) * scale
            potential[:, columns] = value
            factor = data_u[0, t] + data_z[0, t].astype(F32)
            residual = factor * value - (data_u[1, t] + data_z[1, t].astype(F32))
            block[:, inner] = residual.astype(BF16)
            if t < N:
                post[t, 1] = value
            elif t < 2 * N:
                post[t - N, 0] = value
        box["four"] = [start(block, block, box["inner_peer"](d)) for d in FAR_FIRST]
    face_copies += send_faces(2)
    post_copies = begin_y(post, post_y, (None, z == 1))
    for box in streams:
        for copy in box["four"]:
            copy.wait_recv()
        block = box["gather"].at[box["outer"]]
        box["five"] = [start(block, block, box["outer_peer"](d)) for d in FAR_FIRST]
    post_copies = begin_x(post_copies, post_y, post_t, post_x, (None, z == 1))

    total[...] = jnp.zeros_like(total)

    def collect(matrix, columns, pieces):
        count = matrix.shape[0]
        for k in range(3):
            span = slice(k * cells, (k + 1) * cells)
            made = jnp.dot(matrix, grads[columns, span], preferred_element_type=F32)
            rows = [grads[piece, span] for piece in pieces]
            rows = rows[0] if len(rows) == 1 else jnp.concatenate(rows, axis=0)
            made = made * rows.astype(F32)
            total[:, span] += jnp.sum(made.reshape(count // 8, 8, cells), axis=0)

    none = jnp.zeros((tile, LANES), BF16)

    def stack(rows):
        return jnp.concatenate([jnp.concatenate(row, axis=1) for row in rows], axis=0)

    def add_a(box):
        first = half + box["tiles"][0] * LANES
        pieces = [
            slice(yy * tile + xx * own, yy * tile + (xx + 1) * own)
            for xx in range(N)
            for yy in range(N)
        ]
        matrix = box["gather"][...].reshape(half, box["width"])
        collect(matrix, slice(first, first + box["width"]), pieces)

    def tiles_of(box):
        found = {}
        for yy in range(N):
            rows = box["gather"][yy].reshape(tile, box["width"])
            for n, t in enumerate(box["tiles"]):
                found[yy, t] = rows[:, n * LANES : (n + 1) * LANES]
        return found

    def add_b(box):
        f = tiles_of(box)
        if box["tiles"][0] == 0:
            collect(stack([[f[0, 0], f[0, 1]], [none, f[1, 1]]]), slice(0, 256), [slice(0, 256)])
            collect(
                stack([[f[1, 0], none], [f[2, 0], f[2, 1]], [f[3, 0], f[3, 1]]]),
                slice(half, half + 256),
                [slice(half + tile, electrodes)],
            )
        else:
            collect(
                stack([[f[0, 2], f[0, 3]], [f[1, 2], f[1, 3]], [f[2, 2], f[2, 3]], [none, f[3, 3]]]),
                slice(256, half),
                [slice(0, half)],
            )
            collect(
                stack([[f[0, N], none], [none, f[1, N]]]),
                slice(half, half + 256),
                [slice(half, half + 256)],
            )
            collect(
                stack([[f[2, N], none], [f[3, 2], f[3, N]]]),
                slice(half + 256, electrodes),
                [slice(half + 256, electrodes)],
            )

    def finish_misfit():
        for copy in post_copies:
            copy.wait_recv()
        for n in range(2 * N):
            columns = slice(n * LANES, (n + 1) * LANES)
            t = n % N
            between = potential[:, t * LANES : (t + 1) * LANES]
            within = potential[:, half + t * LANES : half + (t + 1) * LANES]
            corner = potential[:, 2 * half : 2 * half + LANES]
            turned = mirrored(post_x, 0, t)
            upper = jnp.where(y <= t, within, turned)
            lower = jnp.where(y > t, within, jnp.where(y == t, corner, turned))
            mine = jnp.where(low, upper, lower)
            others = jnp.where(low, between, mirrored(post_x, 1, t))
            here = low if n < N else z == 1
            value = jnp.where(here, mine, others)
            misfit_out[0, :, columns] = weight[0, :, columns] * (value - observed[0, :, columns])

    for n, ((kind, _), box) in enumerate(zip(STREAMS, streams)):
        for copy in box["five"]:
            copy.wait_recv()
        if kind == "a":
            add_a(box)
        else:
            add_b(box)
        if n == 3:
            finish_misfit()

    for copy in face_copies:
        copy.wait_recv()
    centre = model[0]
    height, width = centre.shape
    lane = lax.broadcasted_iota(jnp.int32, centre.shape, 1)
    zero = jnp.zeros_like(centre)
    before_t = jnp.where(tm > 0, faces[0], zero)
    after_t = jnp.where(tm < times - 1, faces[1], zero)
    before_s = jnp.where(sub > 0, faces[2], zero)
    after_s = jnp.where(sub < parts - 1, faces[3], zero)
    near = after_t + before_t
    near = near + jnp.concatenate([centre[1:], after_s[:1]], axis=0)
    near = near + jnp.concatenate([before_s[height - 1 :], centre[: height - 1]], axis=0)
    near = near + jnp.where(lane == width - 1, 0.0, pltpu.roll(centre, width - 1, 1))
    near = near + jnp.where(lane == 0, 0.0, pltpu.roll(centre, 1, 1))
    smooth = 6.0 * centre - near
    flat = jnp.sum(total[...], axis=0, keepdims=True)
    flat = (flat[:, :cells] + flat[:, cells : 2 * cells] + flat[:, 2 * cells :]) * scale
    for j in range(height):
        gradient_out[0, j : j + 1, :] = flat[:, j * width : (j + 1) * width] + smooth[j : j + 1]

    for copy in sent:
        copy.wait_send()


def body(field_grads, model, observed, data_weight):
    electrodes = field_grads.shape[2]
    columns = field_grads.shape[3]
    width = field_grads.shape[4]
    terms = 3 * columns * width
    own = observed.shape[1]
    half = electrodes // 2
    boxes = []
    for _, tiles in STREAMS:
        w = len(tiles) * LANES
        boxes += [
            pltpu.VMEM((N, N, own, w), F32),
            pltpu.VMEM((N, N, own, w), BF16),
            pltpu.VMEM((3, N, own, w), BF16),
            pltpu.VMEM((N, own, w), F32),
            pltpu.VMEM((3, own, w), F32),
            pltpu.VMEM((own, w), BF16),
            pltpu.VMEM((own, w), BF16),
            pltpu.VMEM((N, N, own, w), BF16),
        ]
    dma = pltpu.SemaphoreType.DMA
    vmem = pl.BlockSpec(memory_space=pltpu.VMEM)
    return pl.pallas_call(
        kernel,
        out_shape=(
            jax.ShapeDtypeStruct(observed.shape, F32),
            jax.ShapeDtypeStruct(model.shape, F32),
        ),
        in_specs=[pl.BlockSpec(memory_space=pltpu.HBM)] * 4,
        out_specs=(vmem, vmem),
        scratch_shapes=[
            pltpu.VMEM(model.shape, F32),
            pltpu.VMEM(observed.shape, F32),
            pltpu.VMEM(observed.shape, F32),
            pltpu.VMEM((3, electrodes, columns, width), BF16),
            pltpu.VMEM((electrodes, terms), BF16),
            pltpu.VMEM((electrodes, terms), BF16),
            pltpu.VMEM((N, 4, own, LANES), F32),
            pltpu.VMEM((N, 4, own, LANES), BF16),
            pltpu.VMEM((N, 4, own, LANES), BF16),
            pltpu.VMEM((N, 4, own, LANES), BF16),
            pltpu.VMEM((N, 4, own, LANES), BF16),
            pltpu.VMEM((2, 2 * N + 1, own, LANES), F32),
            pltpu.VMEM((2, 2 * N + 1, own, LANES), BF16),
            pltpu.VMEM((2, 2 * N + 1, own, LANES), BF16),
            pltpu.VMEM((N, 2, own, LANES), F32),
            pltpu.VMEM((N, 2, own, LANES), F32),
            pltpu.VMEM((N, 2, own, LANES), F32),
            pltpu.VMEM((N, 2, own, LANES), F32),
            pltpu.VMEM((own, 2 * half + LANES), F32),
            pltpu.VMEM((8, terms), F32),
            pltpu.VMEM((4, columns, width), F32),
            dma((6,)),
            dma((80,)),
            dma((80,)),
            pltpu.SemaphoreType.REGULAR,
        ]
        + boxes,
        compiler_params=pltpu.CompilerParams(
            collective_id=0, has_side_effects=True, vmem_limit_bytes=64 * 1024 * 1024 - 65536
        ),
    )(field_grads, model, observed, data_weight)


def solution(mesh):
    return jax.shard_map(
        body,
        mesh=mesh,
        in_specs=(
            P("tm", None, None, "sub", None),
            P("tm", "sub", None),
            P("tm", "sub", None),
            P("tm", "sub", None),
        ),
        out_specs=(P("tm", "sub", None), P("tm", "sub", None)),
        check_vma=False,
    )
```

```python
import jax
import jax.numpy as jnp
from jax import lax
from jax.experimental import pallas as pl
from jax.experimental.pallas import tpu as pltpu
from jax.sharding import PartitionSpec as P

MESH = pl.DeviceIdType.MESH
F32 = jnp.float32
BF16 = jnp.bfloat16
N = 4
NZ = 2
LANES = 128
FAR_FIRST = (2, 1, 3)
STREAMS = (("b", (0, 1)), ("a", (0, 1)), ("b", (2, 3)), ("a", (2, 3)), ("b", (4,)))
BOXES = ("pairs", "send", "recv", "acc", "recv2", "z_send", "z_recv", "gather")


class Copy:
    def __init__(self, copy, sends, receives):
        self.copy = copy
        self.sends = sends
        self.receives = receives

    def start(self):
        when(self.sends, self.copy.start)

    def wait_send(self):
        when(self.sends, self.copy.wait_send)

    def wait_recv(self):
        when(self.receives, self.copy.wait_recv)


def when(condition, action):
    if condition is None:
        action()
    else:

        @pl.when(condition)
        def _():
            action()


def kernel(
    fields,
    model_in,
    observed_in,
    weight_in,
    misfit_out,
    gradient_out,
    model,
    observed,
    weight,
    raw,
    grads,
    weighted,
    direct,
    data,
    data_y,
    data_t,
    data_x,
    data_u,
    data_b,
    data_z,
    post,
    post_y,
    post_t,
    post_x,
    potential,
    total,
    faces,
    load_sem,
    send_sem,
    recv_sem,
    plane_sem,
    *boxes,
):
    electrodes, terms = grads.shape
    half = electrodes // 2
    own = misfit_out.shape[1]
    tile = N * own
    cells = terms // 3
    parts = N * N * NZ
    tm = lax.axis_index("tm")
    sub = lax.axis_index("sub")
    times = lax.axis_size("tm")
    x = lax.rem(sub, N)
    y = lax.rem(sub // N, N)
    z = sub // (N * N)

    def at(zz, yy, xx):
        return {"sub": (zz * N + yy) * N + xx}

    def x_peer(d):
        return at(z, y, lax.rem(x + d, N))

    def y_peer(d):
        return at(z, lax.rem(y + d, N), x)

    z_peer = at(1 - z, y, x)
    beside = (
        ({"tm": lax.rem(tm + 1, times)}, tm < times - 1, tm > 0),
        ({"tm": lax.rem(tm + times - 1, times)}, tm > 0, tm < times - 1),
        ({"sub": lax.rem(sub + 1, parts)}, sub < parts - 1, sub > 0),
        ({"sub": lax.rem(sub + parts - 1, parts)}, sub > 0, sub < parts - 1),
    )
    sent = []

    def start(src, dst, peer, sends=None, receives=None):
        n = len(sent)
        copy = Copy(
            pltpu.make_async_remote_copy(
                src_ref=src,
                dst_ref=dst,
                send_sem=send_sem.at[n],
                recv_sem=recv_sem.at[n],
                device_id=peer,
                device_id_type=MESH,
            ),
            sends,
            receives,
        )
        sent.append(copy)
        copy.start()
        return copy

    loads = [pltpu.make_async_copy(fields.at[0, k], raw.at[k], load_sem.at[k]) for k in range(3)]
    inputs = [
        pltpu.make_async_copy(src, dst, load_sem.at[3 + n])
        for n, (src, dst) in enumerate(
            ((weight_in, weight), (observed_in, observed), (model_in, model))
        )
    ]
    for load in inputs + loads:
        load.start()

    barrier = pltpu.get_barrier_semaphore()
    plane = [x_peer(d) for d in FAR_FIRST] + [y_peer(d) for d in FAR_FIRST]

    def greet(peer, condition=None):
        when(
            condition,
            lambda: pl.semaphore_signal(barrier, inc=1, device_id=peer, device_id_type=MESH),
        )

    greet(z_peer, z == 0)
    for peer in plane:
        greet(peer)
    for peer, condition, _ in beside[:2]:
        greet(peer, condition)
    greetings = len(plane) + z + jnp.where(tm > 0, 1, 0) + jnp.where(tm < times - 1, 1, 0)

    for load in inputs:
        load.wait()

    for n in range(2 * N):
        columns = slice(n * LANES, (n + 1) * LANES)
        e = weight[0, :, columns] * weight[0, :, columns]
        other = z if n < N else 1 - z
        direct[n % N, other] = e
        direct[n % N, 2 + other] = e * observed[0, :, columns]
    data[...] = direct[...].astype(BF16)

    def begin_y(box, box_y, conditions):
        copies = exchange(box, box_y, y, y_peer, conditions)
        box_y[y] = box[y]
        return copies

    def begin_x(copies, box_y, box_t, box_x, conditions):
        for copy in copies:
            copy.wait_recv()
        for q in range(box_y.shape[1]):
            square = jnp.concatenate([box_y[n, q].astype(F32) for n in range(N)], axis=0)
            turned = square.T
            for n in range(N):
                box_t[n, q] = turned[n * own : (n + 1) * own].astype(box_t.dtype)
        copies = exchange(box_t, box_x, x, x_peer, conditions)
        box_x[x] = box_t[x]
        return copies

    def exchange(src, dst, mine, peer_of, conditions):
        if conditions is None:
            return [start(src.at[lax.rem(mine + d, N)], dst.at[mine], peer_of(d)) for d in FAR_FIRST]
        return [
            start(src.at[lax.rem(mine + d, N), q], dst.at[mine, q], peer_of(d), condition, condition)
            for q, condition in enumerate(conditions)
            for d in FAR_FIRST
        ]

    lane_block = lax.broadcasted_iota(jnp.int32, (own, LANES), 1) // own

    def mirrored(box_x, q, t):
        result = None
        for n in range(N):
            moved = box_x[n, q].astype(F32)
            if n != t:
                moved = pltpu.roll(moved, ((n - t) % N) * own, 1)
            result = moved if result is None else jnp.where(lane_block == n, moved, result)
        return result

    cell_row = jnp.concatenate([model[0, j : j + 1, :] for j in range(model.shape[1])], axis=1)

    def lay_out(k):
        loads[k].wait()
        columns = slice(k * cells, (k + 1) * cells)
        for n in range(4):
            rows = slice(n * 256, (n + 1) * 256)
            flat = raw[k, rows].reshape(256, cells)
            grads[rows, columns] = flat
            weighted[rows, columns] = (flat.astype(F32) * cell_row).astype(BF16)

    def product(rows, columns):
        return lax.dot_general(
            weighted[rows, :], grads[columns, :], (((1,), (1,)), ((), ())), preferred_element_type=F32
        )

    streams = []
    for n, (kind, tiles) in enumerate(STREAMS):
        box = dict(zip(BOXES, boxes[len(BOXES) * n : len(BOXES) * (n + 1)]))
        if kind == "a":
            box.update(outer=x, inner=y, outer_peer=x_peer, inner_peer=y_peer)
        else:
            box.update(outer=y, inner=x, outer_peer=y_peer, inner_peer=x_peer)
        box.update(tiles=tiles, first=N * (kind == "b") + tiles[0], width=len(tiles) * LANES)
        streams.append(box)

    lay_out(0)
    pl.semaphore_wait(barrier, greetings)
    when(
        z == 1,
        lambda: pl.semaphore_signal(plane_sem, inc=1, device_id=z_peer, device_id_type=MESH),
    )
    data_copies = begin_y(data, data_y, None)

    def send_faces(first):
        return [
            start(model.at[0], faces.at[first + n], *beside[first + n]) for n in range(2)
        ]

    face_copies = send_faces(0)
    lay_out(1)
    lay_out(2)

    def send_out(kind):
        for (which, _), box in zip(STREAMS, streams):
            if which == kind:
                box["one"] = [
                    start(box["send"].at[lax.rem(box["outer"] + d, N)], box["recv"].at[d - 1], box["outer_peer"](d))
                    for d in FAR_FIRST
                ]

    def keep_at(kind, outer, inner, place, piece):
        for (which, tiles), box in zip(STREAMS, streams):
            if which == kind and place in tiles:
                columns = slice((place - tiles[0]) * LANES, (place - tiles[0] + 1) * LANES)
                box["pairs"][outer, inner, :, columns] = piece
                box["send"][outer, inner, :, columns] = piece.astype(BF16)

    def keep(block, block_row, block_column, row, column, place):
        r = (row - block_row) * LANES
        c = (column - block_column) * LANES
        piece = block[r : r + LANES, c : c + LANES]
        for xx in range(N):
            keep_at("b", row, xx, place, piece[xx * own : (xx + 1) * own])

    for b in range(2):
        upper = product(slice(b * 256, (b + 1) * 256), slice(b * 256, half))
        lower = product(
            slice(half + b * 256, half + (b + 1) * 256), slice(half, half + (b + 1) * 256)
        )
        for row in (2 * b, 2 * b + 1):
            for column in range(N):
                if column >= row:
                    keep(upper, 2 * b, 2 * b, row, column, column)
                else:
                    keep(lower, 2 * b, 0, row, column, column)
            keep(lower, 2 * b, 0, row, row, N)
    send_out("b")
    data_copies = begin_x(data_copies, data_y, data_t, data_x, None)

    for b in range(2):
        block = product(slice(b * 256, (b + 1) * 256), slice(half, electrodes))
        for n in range(2):
            for xx in range(N):
                piece = block[n * tile + xx * own : n * tile + (xx + 1) * own]
                for t in range(N):
                    keep_at("a", xx, 2 * b + n, t, piece[:, t * LANES : (t + 1) * LANES])
    send_out("a")

    for copy in data_copies:
        copy.wait_recv()
    low = z == 0
    nil = jnp.zeros((own, LANES), F32)
    for v in range(2):
        for t in range(N):
            data_u[v, t] = jnp.where(low, direct[t, 2 * v + 1], mirrored(data_x, 2 * v + 1, t))
            plain = direct[t, 2 * v]
            both = plain + mirrored(data_x, 2 * v, t)
            inside = jnp.where(low, t > y, t < y)
            corner = jnp.logical_and(low, y == t)
            data_u[v, N + t] = jnp.where(inside, both, jnp.where(corner, plain, nil))
        data_u[v, 2 * N] = jnp.where(low, nil, direct[y, 2 * v])
    data_b[...] = data_u[...].astype(BF16)
    when(z == 0, lambda: pl.semaphore_wait(plane_sem, 1))
    data_copy = start(data_b, data_z, z_peer)

    def arrived(copies, box):
        for copy in copies:
            copy.wait_recv()
        return box[0].astype(F32) + box[1].astype(F32) + box[2].astype(F32)

    for box in streams:
        box["acc"][...] = box["pairs"][box["outer"]] + arrived(box["one"], box["recv"])
        box["two"] = [
            start(box["acc"].at[lax.rem(box["inner"] + d, N)], box["recv2"].at[d - 1], box["inner_peer"](d))
            for d in FAR_FIRST
        ]
    for box in streams:
        summed = box["acc"][box["inner"]] + arrived(box["two"], box["recv2"])
        potential[:, box["first"] * LANES : box["first"] * LANES + box["width"]] = summed
        box["z_send"][...] = summed.astype(BF16)
        box["three"] = start(box["z_send"], box["z_recv"], z_peer)

    scale = 1.0 / jnp.sqrt(F32(cells * 3 * parts))
    data_copy.wait_recv()

    for box in streams:
        box["three"].wait_recv()
        block = box["gather"].at[box["outer"], box["inner"]]
        for n in range(len(box["tiles"])):
            t = box["first"] + n
            columns = slice(t * LANES, (t + 1) * LANES)
            inner = slice(n * LANES, (n + 1) * LANES)
            value = (potential[:, columns] + box["z_recv"][:, inner].astype(F32)) * scale
            potential[:, columns] = value
            factor = data_u[0, t] + data_z[0, t].astype(F32)
            residual = factor * value - (data_u[1, t] + data_z[1, t].astype(F32))
            block[:, inner] = residual.astype(BF16)
            if t < N:
                post[t, 1] = value
            elif t < 2 * N:
                post[t - N, 0] = value
        box["four"] = [start(block, block, box["inner_peer"](d)) for d in FAR_FIRST]
    face_copies += send_faces(2)
    post_copies = []
    for d in FAR_FIRST:
        to, source = lax.rem(y + d, N), lax.rem(y + N - d, N)
        post_copies.append(
            start(
                post.at[to, 0],
                post_y.at[y, 0],
                y_peer(d),
                jnp.where(low, to - y, y - to) > 0,
                jnp.where(low, y - source, source - y) > 0,
            )
        )
        post_copies.append(start(post.at[to, 1], post_y.at[y, 1], y_peer(d), z == 1, z == 1))
    post_y[y] = post[y]
    for box in streams:
        for copy in box["four"]:
            copy.wait_recv()
        block = box["gather"].at[box["outer"]]
        box["five"] = [start(block, block, box["outer_peer"](d)) for d in FAR_FIRST]
    post_copies = begin_x(post_copies, post_y, post_t, post_x, (None, z == 1))

    total[...] = jnp.zeros_like(total)

    def collect(matrix, columns, pieces):
        count = matrix.shape[0]
        for k in range(3):
            span = slice(k * cells, (k + 1) * cells)
            made = jnp.dot(matrix, grads[columns, span], preferred_element_type=F32)
            rows = [grads[piece, span] for piece in pieces]
            rows = rows[0] if len(rows) == 1 else jnp.concatenate(rows, axis=0)
            made = made * rows.astype(F32)
            total[:, span] += jnp.sum(made.reshape(count // 8, 8, cells), axis=0)

    none = jnp.zeros((tile, LANES), BF16)

    def stack(rows):
        return jnp.concatenate([jnp.concatenate(row, axis=1) for row in rows], axis=0)

    def add_a(box):
        first = half + box["tiles"][0] * LANES
        pieces = [
            slice(yy * tile + xx * own, yy * tile + (xx + 1) * own)
            for xx in range(N)
            for yy in range(N)
        ]
        matrix = box["gather"][...].reshape(half, box["width"])
        collect(matrix, slice(first, first + box["width"]), pieces)

    def tiles_of(box):
        found = {}
        for yy in range(N):
            rows = box["gather"][yy].reshape(tile, box["width"])
            for n, t in enumerate(box["tiles"]):
                found[yy, t] = rows[:, n * LANES : (n + 1) * LANES]
        return found

    def add_b(box):
        f = tiles_of(box)
        if box["tiles"][0] == 0:
            collect(stack([[f[0, 0], f[0, 1]], [none, f[1, 1]]]), slice(0, 256), [slice(0, 256)])
            collect(
                stack([[f[1, 0], none], [f[2, 0], f[2, 1]], [f[3, 0], f[3, 1]]]),
                slice(half, half + 256),
                [slice(half + tile, electrodes)],
            )
        elif box["tiles"][0] == 2:
            collect(
                stack([[f[0, 2], f[0, 3]], [f[1, 2], f[1, 3]], [f[2, 2], f[2, 3]], [none, f[3, 3]]]),
                slice(256, half),
                [slice(0, half)],
            )
            collect(f[3, 2], slice(half + 256, half + 384), [slice(half + 384, electrodes)])
        else:
            collect(
                stack([[f[0, N], none], [none, f[1, N]]]),
                slice(half, half + 256),
                [slice(half, half + 256)],
            )
            collect(
                stack([[f[2, N], none], [none, f[3, N]]]),
                slice(half + 256, electrodes),
                [slice(half + 256, electrodes)],
            )

    def finish_misfit():
        for copy in post_copies:
            copy.wait_recv()
        for n in range(2 * N):
            columns = slice(n * LANES, (n + 1) * LANES)
            t = n % N
            between = potential[:, t * LANES : (t + 1) * LANES]
            within = potential[:, half + t * LANES : half + (t + 1) * LANES]
            corner = potential[:, 2 * half : 2 * half + LANES]
            turned = mirrored(post_x, 0, t)
            upper = jnp.where(y <= t, within, turned)
            lower = jnp.where(y > t, within, jnp.where(y == t, corner, turned))
            mine = jnp.where(low, upper, lower)
            others = jnp.where(low, between, mirrored(post_x, 1, t))
            here = low if n < N else z == 1
            value = jnp.where(here, mine, others)
            misfit_out[0, :, columns] = weight[0, :, columns] * (value - observed[0, :, columns])

    for n, ((kind, _), box) in enumerate(zip(STREAMS, streams)):
        for copy in box["five"]:
            copy.wait_recv()
        if kind == "a":
            add_a(box)
        else:
            add_b(box)
        if n == 4:
            finish_misfit()

    for copy in face_copies:
        copy.wait_recv()
    centre = model[0]
    height, width = centre.shape
    lane = lax.broadcasted_iota(jnp.int32, centre.shape, 1)
    zero = jnp.zeros_like(centre)
    before_t = jnp.where(tm > 0, faces[0], zero)
    after_t = jnp.where(tm < times - 1, faces[1], zero)
    before_s = jnp.where(sub > 0, faces[2], zero)
    after_s = jnp.where(sub < parts - 1, faces[3], zero)
    near = after_t + before_t
    near = near + jnp.concatenate([centre[1:], after_s[:1]], axis=0)
    near = near + jnp.concatenate([before_s[height - 1 :], centre[: height - 1]], axis=0)
    near = near + jnp.where(lane == width - 1, 0.0, pltpu.roll(centre, width - 1, 1))
    near = near + jnp.where(lane == 0, 0.0, pltpu.roll(centre, 1, 1))
    smooth = 6.0 * centre - near
    flat = jnp.sum(total[...], axis=0, keepdims=True)
    flat = (flat[:, :cells] + flat[:, cells : 2 * cells] + flat[:, 2 * cells :]) * scale
    for j in range(height):
        gradient_out[0, j : j + 1, :] = flat[:, j * width : (j + 1) * width] + smooth[j : j + 1]

    for copy in sent:
        copy.wait_send()


def body(field_grads, model, observed, data_weight):
    electrodes = field_grads.shape[2]
    columns = field_grads.shape[3]
    width = field_grads.shape[4]
    terms = 3 * columns * width
    own = observed.shape[1]
    half = electrodes // 2
    boxes = []
    for _, tiles in STREAMS:
        w = len(tiles) * LANES
        boxes += [
            pltpu.VMEM((N, N, own, w), F32),
            pltpu.VMEM((N, N, own, w), BF16),
            pltpu.VMEM((3, N, own, w), BF16),
            pltpu.VMEM((N, own, w), F32),
            pltpu.VMEM((3, own, w), F32),
            pltpu.VMEM((own, w), BF16),
            pltpu.VMEM((own, w), BF16),
            pltpu.VMEM((N, N, own, w), BF16),
        ]
    dma = pltpu.SemaphoreType.DMA
    vmem = pl.BlockSpec(memory_space=pltpu.VMEM)
    return pl.pallas_call(
        kernel,
        out_shape=(
            jax.ShapeDtypeStruct(observed.shape, F32),
            jax.ShapeDtypeStruct(model.shape, F32),
        ),
        in_specs=[pl.BlockSpec(memory_space=pltpu.HBM)] * 4,
        out_specs=(vmem, vmem),
        scratch_shapes=[
            pltpu.VMEM(model.shape, F32),
            pltpu.VMEM(observed.shape, F32),
            pltpu.VMEM(observed.shape, F32),
            pltpu.VMEM((3, electrodes, columns, width), BF16),
            pltpu.VMEM((electrodes, terms), BF16),
            pltpu.VMEM((electrodes, terms), BF16),
            pltpu.VMEM((N, 4, own, LANES), F32),
            pltpu.VMEM((N, 4, own, LANES), BF16),
            pltpu.VMEM((N, 4, own, LANES), BF16),
            pltpu.VMEM((N, 4, own, LANES), BF16),
            pltpu.VMEM((N, 4, own, LANES), BF16),
            pltpu.VMEM((2, 2 * N + 1, own, LANES), F32),
            pltpu.VMEM((2, 2 * N + 1, own, LANES), BF16),
            pltpu.VMEM((2, 2 * N + 1, own, LANES), BF16),
            pltpu.VMEM((N, 2, own, LANES), F32),
            pltpu.VMEM((N, 2, own, LANES), F32),
            pltpu.VMEM((N, 2, own, LANES), F32),
            pltpu.VMEM((N, 2, own, LANES), F32),
            pltpu.VMEM((own, 2 * half + LANES), F32),
            pltpu.VMEM((8, terms), F32),
            pltpu.VMEM((4, columns, width), F32),
            dma((6,)),
            dma((96,)),
            dma((96,)),
            pltpu.SemaphoreType.REGULAR,
        ]
        + boxes,
        compiler_params=pltpu.CompilerParams(
            collective_id=0, has_side_effects=True, vmem_limit_bytes=64 * 1024 * 1024 - 65536
        ),
    )(field_grads, model, observed, data_weight)


def solution(mesh):
    return jax.shard_map(
        body,
        mesh=mesh,
        in_specs=(
            P("tm", None, None, "sub", None),
            P("tm", "sub", None),
            P("tm", "sub", None),
            P("tm", "sub", None),
        ),
        out_specs=(P("tm", "sub", None), P("tm", "sub", None)),
        check_vma=False,
    )
```
